32 devices in a mesh: grp: 2 (over y), bl: 4 (over z), ch: 2 (over x), pol: 2 (over core).
Axes of the slice: x: 2, y: 2, z: 4, core: 2. Of those that a mesh axis runs over, the one named last changes fastest.
Arguments:
- visibility: float32 [4, 2, 2, 384, 1024], P('pol', None, None, 'ch', ('grp', 'bl')), parts along dimension 4, may hold values from -6 to 6
- uv_coords: float32 [2, 2, 1024], P(None, None, ('grp', 'bl')), parts along dimension 2, may hold values from -3072 to 3072
- source_lm: float32 [2, 64], replicated, may hold values from -0.1 to 0.1
- source_flux: float32 [4, 64], P('pol'), may hold values from -1 to 1
- avg_factor: int32 [1024], P(('grp', 'bl')), parts along dimension 0, may hold values from 1 to 2, as said below
- station_pairs: int32 [2, 1024], P(None, ('grp', 'bl')), parts along dimension 1, may hold values from 0 to 511, as said below
- slot_owner: int32 [2], replicated, may hold values from 0 to 1, each once
Outputs:
- residual: float32 [4, 2, 2, 384, 1024], P('pol', None, 'ch', None, ('grp', 'bl')), parts along dimension 4
- gains: float32 [3, 2, 2, 1024], P(None, None, 'ch', 'grp'), parts along dimension 3
The draws below stay inside these ranges and needn't reach their ends.
There are 2 independent parts, one for each index of `grp`. The reference program is written for one: setup_inputs(seed, part) draws one part's arguments, and reference() takes and returns one part's arrays. A program takes and returns all parts, laid end to end along the dimension named above; an argument that names none is the same for every part. Nothing has to cross between parts.
Inputs may be any that keep to these rules, and one draw needn't show every extreme that they name: `avg_factor`: each factor is a power of two. `station_pairs`: the two stations of a baseline differ; the first stations of the baselines in aligned blocks of 128 rows lie in the matching block of 128 stations. `slot_owner`: each position occurs once.
All inputs are finite; a program needn't handle non-finite values.
Results may differ from the reference program's by a relative error of at most 0.0003.
Values sent between devices are 32-bit elements; how exact they have to be, the bound alone decides.
A program may use at most 64 MiB of HBM per device.

```python
import jax
import jax.numpy as jnp
from jax import lax

STATIONS = 512
CHAN = 384
BL_DEV = 128
SOURCES = 64
SRC_BLOCK = 16
ITERS = 3
SLOTS = 2
NBL = 512


def draw_avg_factor(key, part):
    key = jax.random.fold_in(key, 11)
    top_power = SLOTS.bit_length() - 1
    exponent = jax.random.randint(key, (NBL,), 0, top_power + 1).astype(jnp.int32)
    factor = jnp.left_shift(jnp.ones((NBL,), jnp.int32), exponent)
    factor = factor.at[0].set(SLOTS).at[1].set(1)
    return factor.astype(jnp.int32)


def draw_station_pairs(key, part):
    key = jax.random.fold_in(key, 23)
    first_key, second_key = jax.random.split(key)
    blocks = NBL // BL_DEV
    block_width = STATIONS // blocks
    row_index = jnp.arange(NBL, dtype=jnp.int32)
    first_station = row_index // BL_DEV * block_width + jax.random.randint(first_key, (NBL,), 0, block_width).astype(jnp.int32)
    first_station = first_station.at[0].set(0)
    second = (first_station + 1 + jax.random.randint(second_key, (NBL,), 0, STATIONS - 1).astype(jnp.int32)) % STATIONS
    second = second.at[0].set(STATIONS - 1)
    return jnp.stack([first_station, second]).astype(jnp.int32)


def shard_levels(stream_key, extent, shards, low, high):
    level, own = 1.0, jax.random.fold_in(stream_key, 6)
    for axis_at, shards_of in shards:
        steps = jnp.exp(jax.random.uniform(jax.random.fold_in(own, axis_at), (shards_of,), jnp.float32, low / len(shards), high / len(shards)))
        level = level * jnp.repeat(steps, extent[axis_at] // shards_of).reshape([-1 if axis == axis_at else 1 for axis in range(len(extent))])
    return level


def noise(own_key, shape, spread, bound, shards=(), kind=jnp.bfloat16):
    drawn = jax.random.normal(own_key, shape, jnp.float32) * spread
    if len(shards) > 0:
        drawn = shard_levels(own_key, shape, shards, -0.22, 0.18) * drawn
    return jnp.clip(drawn, min=-bound, max=bound).astype(kind)


def setup_inputs(seed: int = 0, part: int = 0) -> dict:
    key_list = jax.random.split(jax.random.key(seed), 8)
    own_keys = jax.random.split(jax.random.fold_in(key_list[7], part), 8)
    return {
        "visibility": noise(own_keys[0], (4, 2, SLOTS, CHAN, NBL), 1.0, 6.0, ((0, 2), (3, 2), (4, 4)), jnp.float32),
        "uv_coords": noise(own_keys[1], (2, SLOTS, NBL), 500.0, 3072.0, ((2, 4),), jnp.float32),
        "source_lm": jnp.clip(jax.random.uniform(key_list[2], (2, SOURCES), jnp.float32, -0.1, 0.1), -0.1, 0.1),
        "source_flux": noise(key_list[3], (4, SOURCES), 0.125, 1.0, ((0, 2),), jnp.float32),
        "avg_factor": draw_avg_factor(jax.random.fold_in(jax.random.fold_in(key_list[7], part), 71), part),
        "station_pairs": draw_station_pairs(jax.random.fold_in(jax.random.fold_in(key_list[7], part), 71), part),
        "slot_owner": jax.random.permutation(key_list[6], SLOTS).astype(jnp.int32),
    }


damping = 1.0
two_pi = 6.283185307179586
highest = lax.Precision.HIGHEST


def averaging_weights(avg_factor, slot_count):
    slot_index = jnp.arange(slot_count, dtype=jnp.int32)
    factor = avg_factor[None, None, :]
    same_group = (slot_index[:, None, None] // factor) == (slot_index[None, :, None] // factor)
    return same_group.astype(jnp.float32) / factor.astype(jnp.float32)


def owner_slots(slot_owner):
    slot_index = jnp.arange(slot_owner.shape[0], dtype=jnp.int32)
    match_table = slot_owner[:, None] == slot_index[None, :]
    return jnp.sum(jnp.where(match_table, slot_index[:, None], 0), axis=0).astype(jnp.int32)


def predict_slot(uv_slot, source_lm, source_flux, frequency, block_size):
    geometry = source_lm[0][:, None] * uv_slot[0][None, :] + source_lm[1][:, None] * uv_slot[1][None, :]
    start_value = jnp.zeros((source_flux.shape[0], 2, frequency.shape[0], uv_slot.shape[1]), jnp.float32)

    def add_block(block_number, running_total):
        first_source = (block_number * block_size).astype(jnp.int32)
        geo_block = lax.dynamic_slice_in_dim(geometry, first_source, block_size, 0)
        flux_block = lax.dynamic_slice_in_dim(source_flux, first_source, block_size, 1)
        phase_angle = -two_pi * frequency[None, :, None] * geo_block[:, None, :]
        real_part = jnp.einsum("ks,scb->kcb", flux_block, jnp.cos(phase_angle), precision=highest)
        imag_part = jnp.einsum("ks,scb->kcb", flux_block, jnp.sin(phase_angle), precision=highest)
        return running_total + jnp.stack([real_part, imag_part], axis=1)

    return lax.fori_loop(0, geometry.shape[0] // block_size, add_block, start_value)


def averaged_rows(row_weights, slot_values, row_shape):
    def add_slot(slot_number, running_total):
        weight = lax.dynamic_index_in_dim(row_weights, slot_number, 1, keepdims=False)
        return running_total + weight[None, None, :, None, :] * slot_values(slot_number)[:, :, None]

    return lax.fori_loop(0, row_weights.shape[1], add_slot, jnp.zeros(row_shape, jnp.float32))


def model_residual(data_rows, model_rows, gains, first_station, second_station, first_pol, frequency):
    own_pol = lax.dynamic_index_in_dim(gains, first_pol, 1, keepdims=False)
    first_gain = jnp.take(own_pol, first_station, axis=2)[:, None, :, None, :]
    second_gain = jnp.take(gains, second_station, axis=3)[:, :, :, None, :]
    angular = two_pi * frequency[None, None, :, None]
    phase_angle = angular * (first_gain[2] - second_gain[2])
    cos_phase = jnp.cos(phase_angle)
    sin_phase = jnp.sin(phase_angle)
    model_real = model_rows[:, 0]
    model_imag = model_rows[:, 1]
    turned_real = cos_phase * model_real - sin_phase * model_imag
    turned_imag = sin_phase * model_real + cos_phase * model_imag
    conj_real = second_gain[0] * turned_real + second_gain[1] * turned_imag
    conj_imag = second_gain[0] * turned_imag - second_gain[1] * turned_real
    lead_real = first_gain[0] * turned_real - first_gain[1] * turned_imag
    lead_imag = first_gain[0] * turned_imag + first_gain[1] * turned_real
    pred_real = first_gain[0] * conj_real - first_gain[1] * conj_imag
    pred_imag = first_gain[0] * conj_imag + first_gain[1] * conj_real
    resid_real = data_rows[:, 0] - pred_real
    resid_imag = data_rows[:, 1] - pred_imag
    return (resid_real, resid_imag, conj_real, conj_imag, lead_real, lead_imag, pred_real, pred_imag, angular)


def normal_terms(pieces, first_hot, second_hot, first_pol):
    resid_real, resid_imag, conj_real, conj_imag, lead_real, lead_imag, pred_real, pred_imag, angular = pieces
    conj_power = conj_real * conj_real + conj_imag * conj_imag
    lead_power = lead_real * lead_real + lead_imag * lead_imag
    squared = angular * angular
    pred_cross = pred_real * resid_imag - pred_imag * resid_real
    first_terms = jnp.stack([
        jnp.sum(conj_power, axis=(0, 2)),
        jnp.sum(angular * conj_power, axis=(0, 2)),
        jnp.sum(squared * conj_power, axis=(0, 2)),
        jnp.sum(conj_real * resid_real + conj_imag * resid_imag, axis=(0, 2)),
        jnp.sum(conj_real * resid_imag - conj_imag * resid_real, axis=(0, 2)),
        jnp.sum(angular * pred_cross, axis=(0, 2))])
    second_terms = jnp.stack([
        jnp.sum(lead_power, axis=2),
        jnp.sum(angular * lead_power, axis=2),
        jnp.sum(squared * lead_power, axis=2),
        jnp.sum(lead_real * resid_real + lead_imag * resid_imag, axis=2),
        -jnp.sum(lead_real * resid_imag - lead_imag * resid_real, axis=2),
        -jnp.sum(angular * pred_cross, axis=2)])
    first_sums = jnp.einsum("xnb,bs->xns", first_terms, first_hot, precision=highest)
    second_sums = jnp.einsum("xqnb,bs->xqns", second_terms, second_hot, precision=highest)
    select = (jnp.arange(2) == first_pol).astype(jnp.float32)
    return second_sums + first_sums[:, None] * select[None, :, None, None]


def gain_update(gains, normals):
    real_gain = gains[0]
    imag_gain = gains[1]
    delay = gains[2]
    diagonal = (1.0 + damping) * normals[0] + 1.0
    cross_real = -imag_gain * normals[1]
    cross_imag = real_gain * normals[1]
    delay_diag = (1.0 + damping) * (real_gain * real_gain + imag_gain * imag_gain) * normals[2] + 1.0
    step_delay = (diagonal * normals[5] - cross_real * normals[3] - cross_imag * normals[4]) / (
        diagonal * delay_diag - cross_real * cross_real - cross_imag * cross_imag)
    step_real = (normals[3] - cross_real * step_delay) / diagonal
    step_imag = (normals[4] - cross_imag * step_delay) / diagonal
    return jnp.stack([real_gain + step_real, imag_gain + step_imag, delay + step_delay])


def reference(visibility, uv_coords, source_lm, source_flux, avg_factor, station_pairs, slot_owner):
    frequency = 0.5 + (jnp.arange(CHAN, dtype=jnp.float32) + 0.5) / CHAN
    slot_order = owner_slots(slot_owner)
    row_weights = jnp.take(averaging_weights(avg_factor, SLOTS), slot_order, axis=0)
    row_shape = (4, 2, SLOTS, CHAN, NBL)

    def data_slot(slot_number):
        return lax.dynamic_index_in_dim(visibility, slot_number, 2, keepdims=False)

    def model_slot(slot_number):
        uv_slot = lax.dynamic_index_in_dim(uv_coords, slot_number, 1, keepdims=False)
        return predict_slot(uv_slot, source_lm, source_flux, frequency, SRC_BLOCK)

    data_rows = averaged_rows(row_weights, data_slot, row_shape)
    model_rows = averaged_rows(row_weights, model_slot, row_shape)
    first_station = station_pairs[0]
    second_station = station_pairs[1]
    station_index = jnp.arange(STATIONS, dtype=jnp.int32)
    first_hot = (first_station[:, None] == station_index[None, :]).astype(jnp.float32)
    second_hot = (second_station[:, None] == station_index[None, :]).astype(jnp.float32)

    def solve_slot(slot_pair):
        data_slot_rows = slot_pair[0][:, :, None]
        model_slot_rows = slot_pair[1][:, :, None]
        ones_part = jnp.ones((2, 1, STATIONS), jnp.float32)
        zero_part = jnp.zeros((2, 1, STATIONS), jnp.float32)
        gains = jnp.stack([ones_part, zero_part, zero_part])
        for iteration in range(ITERS):
            normals = jnp.zeros((6, 2, 1, STATIONS), jnp.float32)
            for first_pol in range(2):
                pieces = model_residual(data_slot_rows[2 * first_pol:2 * first_pol + 2], model_slot_rows[2 * first_pol:2 * first_pol + 2], gains, first_station, second_station, first_pol, frequency)
                normals = normals + normal_terms(pieces, first_hot, second_hot, first_pol)
            gains = gain_update(gains, normals)
        halves = []
        for first_pol in range(2):
            pieces = model_residual(data_slot_rows[2 * first_pol:2 * first_pol + 2], model_slot_rows[2 * first_pol:2 * first_pol + 2], gains, first_station, second_station, first_pol, frequency)
            halves.append(jnp.stack([pieces[0], pieces[1]], axis=1))
        return jnp.concatenate(halves, axis=0)[:, :, 0], gains[:, :, 0]

    residual, gains = lax.map(solve_slot, (jnp.moveaxis(data_rows, 2, 0), jnp.moveaxis(model_rows, 2, 0)))
    return jnp.moveaxis(residual, 0, 2), jnp.moveaxis(gains, 0, 2)
```

```python
import functools

import jax
import jax.numpy as jnp
from jax import lax
from jax.experimental import pallas as pl
from jax.experimental.pallas import tpu as pltpu
from jax.sharding import PartitionSpec as P

ITERS = 3
LANES = 128
TILE = 4
damping = 1.0
two_pi = 6.283185307179586
MESH = pl.DeviceIdType.MESH

SIN_COEF = (
    3.141592653589793,
    -5.16771278004997,
    2.550164039877345,
    -0.5992645293207921,
    0.08214588661112823,
    -0.00737043094571435,
)
COS_COEF = (
    1.0,
    -4.934802200544679,
    4.058712126416768,
    -1.3352627688545893,
    0.2353306303588935,
    -0.02580689139001406,
    0.0019295743094039231,
)


def sincos_turns(turns):
    part = turns - jnp.floor(turns + 0.5)
    sq = part * part
    sin_half = jnp.full_like(sq, SIN_COEF[-1])
    for coef in SIN_COEF[-2::-1]:
        sin_half = sin_half * sq + coef
    sin_half = sin_half * part
    cos_half = jnp.full_like(sq, COS_COEF[-1])
    for coef in COS_COEF[-2::-1]:
        cos_half = cos_half * sq + coef
    twice = sin_half + sin_half
    return twice * cos_half, 1.0 - twice * sin_half


def split3(value):
    high = value.astype(jnp.bfloat16)
    rest = value - high.astype(jnp.float32)
    mid = rest.astype(jnp.bfloat16)
    low = (rest - mid.astype(jnp.float32)).astype(jnp.bfloat16)
    return jnp.concatenate([high, mid, low], axis=0)


def kernel(
    sizes,
    vis,
    uv,
    lm,
    flux,
    factor,
    pairs,
    owner,
    res_out,
    gains_out,
    vbuf,
    sbuf,
    model,
    geo,
    ftab,
    dtab,
    xtab,
    psend,
    pall,
    mall,
    yall,
    onehot,
    terms,
    gathered,
    v_send,
    v_recv,
    p_send,
    p_recv,
    m_send,
    m_recv,
    y_send,
    y_recv,
):
    ch_count, bl_count, pol_count, slots, chan_local, chans, sources, stations = sizes
    ch = lax.axis_index("ch")
    bl = lax.axis_index("bl")
    pol = lax.axis_index("pol")
    group = bl_count * pol_count
    me = bl * pol_count + pol
    half = chans // 16
    base_all = bl_count * LANES

    def ch_peer(step):
        return lax.rem(ch + step, ch_count)

    def group_peer(step):
        other = lax.rem(me + step, group)
        return {"bl": other // pol_count, "pol": lax.rem(other, pol_count)}

    barrier = pltpu.get_barrier_semaphore()
    for step in range(1, ch_count):
        pl.semaphore_signal(
            barrier, inc=1, device_id={"ch": ch_peer(step)}, device_id_type=MESH
        )
    for step in range(1, group):
        pl.semaphore_signal(barrier, inc=1, device_id=group_peer(step), device_id_type=MESH)

    fac = factor[...]
    inverse = jnp.zeros(fac.shape, jnp.float32)
    power = 1
    while power <= slots:
        inverse = jnp.where(fac == power, jnp.float32(1.0 / power), inverse)
        power *= 2

    def weight_rows(position):
        slot = jnp.int32(0)
        for s in range(slots):
            slot = slot + jnp.where(owner[s] == position, jnp.int32(s), jnp.int32(0))
        return [
            jnp.where(jnp.bitwise_xor(slot, jnp.int32(t)) < fac, inverse, 0.0)
            for t in range(slots)
        ]

    def averaged(rows, k, r):
        total = rows[0] * vis[k, r, 0]
        for t in range(1, slots):
            total = total + rows[t] * vis[k, r, t]
        return total

    for step in range(1, ch_count):
        rows = weight_rows(ch_peer(step))
        for k in range(2):
            for r in range(2):
                sbuf[step - 1, k, r] = averaged(rows, k, r)
    own_rows = weight_rows(ch)
    own_span = pl.ds(pl.multiple_of(ch * chan_local, 8), chan_local)
    for i in range(2):
        psend[pl.ds(i, 1), :] = pairs[pl.ds(i, 1), :]
    psend[pl.ds(2, 6), :] = jnp.zeros((6, LANES), jnp.int32)

    pl.semaphore_wait(barrier, ch_count - 1 + group - 1)

    v_copies = []
    for step in range(1, ch_count):
        copy = pltpu.make_async_remote_copy(
            src_ref=sbuf.at[step - 1],
            dst_ref=vbuf.at[:, :, own_span, :],
            send_sem=v_send.at[step - 1],
            recv_sem=v_recv.at[step - 1],
            device_id={"ch": ch_peer(step)},
            device_id_type=MESH,
        )
        copy.start()
        v_copies.append(copy)
    p_copies = []
    for step in range(1, bl_count):
        copy = pltpu.make_async_remote_copy(
            src_ref=psend,
            dst_ref=pall.at[bl],
            send_sem=p_send.at[step - 1],
            recv_sem=p_recv.at[step - 1],
            device_id={"bl": lax.rem(bl + step, bl_count)},
            device_id_type=MESH,
        )
        copy.start()
        p_copies.append(copy)
    pall[bl] = psend[...]
    for k in range(2):
        for r in range(2):
            vbuf[k, r, own_span, :] = averaged(own_rows, k, r)

    def geo_row(s, _):
        for t in range(slots):
            geo[pl.ds(t * sources + s, 1), :] = -(
                lm[0, s] * uv[0, pl.ds(t, 1), :] + lm[1, s] * uv[1, pl.ds(t, 1), :]
            )
        return 0

    lax.fori_loop(0, sources, geo_row, 0, unroll=8)

    def offset_rows(block, _):
        span = pl.ds(pl.multiple_of(block * 32, 32), 32)
        sin_h, cos_h = sincos_turns(geo[span, :] * jnp.float32(4.0 / chans))
        cos_f = cos_h * cos_h - sin_h * sin_h
        sin_f = 2.0 * sin_h * cos_h
        for d in range(half):
            dtab[d, 0, span, :] = cos_h
            dtab[d, 1, span, :] = sin_h
            cos_h, sin_h = cos_h * cos_f - sin_h * sin_f, sin_h * cos_f + cos_h * sin_f
        return 0

    lax.fori_loop(0, slots * sources // 32, offset_rows, 0)

    sub = lax.broadcasted_iota(jnp.int32, (8, LANES), 0).astype(jnp.float32)
    freq_c = 0.5 + (sub + jnp.float32(4 * (chans // 8 - 1) + 0.5)) / chans
    omega_c = two_pi * freq_c
    omega_step = jnp.float32(two_pi * 8.0 / chans)

    for t in range(slots):
        wide = jnp.broadcast_to(own_rows[t], (8, LANES))

        def centre(s, _, t=t, wide=wide):
            row = t * sources + s
            sin_c, cos_c = sincos_turns(geo[pl.ds(row, 1), :] * freq_c)
            sin_c = sin_c * wide
            cos_c = cos_c * wide
            span = pl.ds(pl.multiple_of(row * 8, 8), 8)
            for k in range(2):
                ftab[k, 0, span, :] = flux[k, s] * cos_c
                ftab[k, 1, span, :] = flux[k, s] * sin_c
            return 0

        lax.fori_loop(0, sources, centre, 0, unroll=4)

    zero = jnp.zeros((8, LANES), jnp.float32)
    moments = [[zero, zero, zero] for _ in range(2)]
    for first in range(0, half, TILE):
        count = min(TILE, half - first)

        def add_source(row, acc, first=first, count=count):
            span = pl.ds(pl.multiple_of(row * 8, 8), 8)
            fc = [ftab[k, 0, span, :] for k in range(2)]
            fs = [ftab[k, 1, span, :] for k in range(2)]
            out = []
            at = 0
            for d in range(count):
                cd = jnp.broadcast_to(dtab[first + d, 0, pl.ds(row, 1), :], (8, LANES))
                sd = jnp.broadcast_to(dtab[first + d, 1, pl.ds(row, 1), :], (8, LANES))
                for k in range(2):
                    out.append(acc[at] + fc[k] * cd)
                    out.append(acc[at + 1] + fs[k] * sd)
                    out.append(acc[at + 2] + fs[k] * cd)
                    out.append(acc[at + 3] + fc[k] * sd)
                    at += 4
            return tuple(out)

        acc = lax.fori_loop(
            0, slots * sources, add_source, (zero,) * (8 * count), unroll=4
        )
        for d in range(count):
            dist = jnp.float32(first + d + 0.5)
            up = pl.ds(8 * (half + first + d), 8)
            down = pl.ds(8 * (half - 1 - first - d), 8)
            for k in range(2):
                cc, ss, sc, cs = acc[(d * 2 + k) * 4 : (d * 2 + k) * 4 + 4]
                up_r, up_i, dn_r, dn_i = cc - ss, sc + cs, cc + ss, sc - cs
                model[k, 0, up, :] = up_r
                model[k, 1, up, :] = up_i
                model[k, 0, down, :] = dn_r
                model[k, 1, down, :] = dn_i
                up_p = up_r * up_r + up_i * up_i
                dn_p = dn_r * dn_r + dn_i * dn_i
                both = up_p + dn_p
                moments[k][0] = moments[k][0] + both
                moments[k][1] = moments[k][1] + dist * (up_p - dn_p)
                moments[k][2] = moments[k][2] + (dist * dist) * both

    def fold(value):
        return jnp.sum(value, axis=0, keepdims=True)

    for k in range(2):
        a0, a1, a2 = moments[k]
        mall[me, pl.ds(k, 1), :] = fold(a0)
        mall[me, pl.ds(2 + k, 1), :] = fold(omega_c * a0 + omega_step * a1)
        mall[me, pl.ds(4 + k, 1), :] = fold(
            omega_c * omega_c * a0
            + 2.0 * omega_step * omega_c * a1
            + omega_step * omega_step * a2
        )
    mall[me, pl.ds(6, 2), :] = jnp.zeros((2, LANES), jnp.float32)

    def spread(block, send_sem, recv_sem):
        copies = []
        for step in range(1, group):
            copy = pltpu.make_async_remote_copy(
                src_ref=block,
                dst_ref=block,
                send_sem=send_sem.at[step - 1],
                recv_sem=recv_sem.at[step - 1],
                device_id=group_peer(step),
                device_id_type=MESH,
            )
            copy.start()
            copies.append(copy)
        return copies

    m_copies = spread(mall.at[me], m_send, m_recv)

    for copy in p_copies:
        copy.wait()
    station = lax.broadcasted_iota(jnp.int32, (stations, LANES), 0)
    for b in range(bl_count):
        for i in range(2):
            hot = (station == pall[b, pl.ds(i, 1), :]).astype(jnp.float32)
            onehot[:, pl.ds(i * base_all + b * LANES, LANES)] = hot.astype(jnp.bfloat16)

    for copy in v_copies:
        copy.wait()

    for d in range(half):
        up = pl.ds(8 * (half + d), 8)
        down = pl.ds(8 * (half - 1 - d), 8)
        at = pl.ds(8 * d, 8)
        for k in range(2):
            halves = []
            for span in (up, down):
                m_r, m_i = model[k, 0, span, :], model[k, 1, span, :]
                v_r, v_i = vbuf[k, 0, span, :], vbuf[k, 1, span, :]
                halves.append((m_r * v_r + m_i * v_i, m_r * v_i - m_i * v_r))
            (u_r, u_i), (l_r, l_i) = halves
            xtab[k, 0, at, :] = u_r + l_r
            xtab[k, 1, at, :] = u_i + l_i
            xtab[k, 2, at, :] = u_r - l_r
            xtab[k, 3, at, :] = u_i - l_i

    own_first = pl.ds(pl.multiple_of(bl * LANES, LANES), LANES)
    own_second = pl.ds(pl.multiple_of(base_all + bl * LANES, LANES), LANES)
    dist_col = lax.broadcasted_iota(jnp.int32, (half, LANES), 0).astype(jnp.float32) + 0.5

    def own_gain(row):
        return jnp.where(
            pol == 0,
            gathered[pl.ds(row, 1), own_first],
            gathered[pl.ds(row + 1, 1), own_first],
        )

    def delay_tables(k):
        tau = own_gain(4) - gathered[pl.ds(4 + k, 1), own_second]
        sin_d, cos_d = sincos_turns(dist_col * (tau * jnp.float32(8.0 / chans)))
        sin_c, cos_c = sincos_turns(freq_c * tau)
        return sin_d, cos_d, sin_c, cos_c

    gains = (
        jnp.ones((2, stations), jnp.float32),
        jnp.zeros((2, stations), jnp.float32),
        jnp.zeros((2, stations), jnp.float32),
    )
    gathered[pl.ds(0, 2), :] = jnp.ones((2, 2 * base_all), jnp.float32)
    gathered[pl.ds(2, 14), :] = jnp.zeros((14, 2 * base_all), jnp.float32)
    terms[pl.ds(12, 4), :] = jnp.zeros((4, 2 * base_all), jnp.float32)

    for it in range(ITERS):
        for k in range(2):
            if it > 0:
                sin_d, cos_d, sin_c, cos_c = delay_tables(k)
            u_r, u_i, w_r, w_i = zero, zero, zero, zero
            for d in range(half):
                at = pl.ds(8 * d, 8)
                p_r, p_i = xtab[k, 0, at, :], xtab[k, 1, at, :]
                m_r, m_i = xtab[k, 2, at, :], xtab[k, 3, at, :]
                dist = jnp.float32(d + 0.5)
                if it > 0:
                    cd, sd = cos_d[d : d + 1, :], sin_d[d : d + 1, :]
                    u_r = u_r + (cd * p_r + sd * m_i)
                    u_i = u_i + (cd * p_i - sd * m_r)
                    cd, sd = dist * cd, dist * sd
                    w_r = w_r + (cd * m_r + sd * p_i)
                    w_i = w_i + (cd * m_i - sd * p_r)
                else:
                    u_r = u_r + p_r
                    u_i = u_i + p_i
                    w_r = w_r + dist * m_r
                    w_i = w_i + dist * m_i
            w_r = omega_c * u_r + omega_step * w_r
            w_i = omega_c * u_i + omega_step * w_i
            if it > 0:
                u_r, u_i = cos_c * u_r + sin_c * u_i, cos_c * u_i - sin_c * u_r
                w_r, w_i = cos_c * w_r + sin_c * w_i, cos_c * w_i - sin_c * w_r
            for n, value in enumerate((u_r, u_i, w_r, w_i)):
                yall[it, me, pl.ds(2 * n + k, 1), :] = fold(value)
        copies = spread(yall.at[it, me], y_send.at[it], y_recv.at[it])
        if it == 0:
            for copy in m_copies:
                copy.wait()
        for copy in copies:
            copy.wait()

        for b in range(bl_count):
            lane_1 = pl.ds(b * LANES, LANES)
            lane_2 = pl.ds(base_all + b * LANES, LANES)
            uj, wj = gathered[pl.ds(0, 2), lane_2], gathered[pl.ds(2, 2), lane_2]
            nj = uj * uj + wj * wj
            second = [jnp.zeros((2, LANES), jnp.float32)] * 6
            for p in range(pol_count):
                dev = b * pol_count + p
                ui, wi = gathered[pl.ds(p, 1), lane_1], gathered[pl.ds(2 + p, 1), lane_1]
                ni = ui * ui + wi * wi
                y0r, y0i, y1r, y1i = [yall[it, dev, pl.ds(2 * n, 2), :] for n in range(4)]
                p0, p1, p2 = [mall[dev, pl.ds(2 * n, 2), :] for n in range(3)]
                b_r = uj * y1r - wj * y1i
                b_i = uj * y1i + wj * y1r
                cross = ui * b_i - wi * b_r
                s0 = nj * p0
                first = (
                    s0,
                    nj * p1,
                    nj * p2,
                    uj * y0r - wj * y0i - ui * s0,
                    uj * y0i + wj * y0r - wi * s0,
                    cross,
                )
                for x in range(6):
                    terms[pl.ds(2 * x + p, 1), lane_1] = fold(first[x])
                t0 = ni * p0
                more = (
                    t0,
                    ni * p1,
                    ni * p2,
                    ui * y0r + wi * y0i - uj * t0,
                    -(ui * y0i - wi * y0r + wj * t0),
                    -cross,
                )
                second = [a + c for a, c in zip(second, more)]
            for x in range(6):
                terms[pl.ds(2 * x, 2), lane_2] = second[x]

        summed = lax.dot_general(
            split3(terms[...]),
            onehot[...],
            (((1,), (1,)), ((), ())),
            preferred_element_type=jnp.float32,
        )
        summed = summed[0:16] + summed[16:32] + summed[32:48]
        s0, s1, s2, g1, g2, g3 = [summed[2 * x : 2 * x + 2] for x in range(6)]
        u, w, tau = gains
        diagonal = (1.0 + damping) * s0 + 1.0
        cross_r = -w * s1
        cross_i = u * s1
        delay_diag = (1.0 + damping) * (u * u + w * w) * s2 + 1.0
        step_d = (diagonal * g3 - cross_r * g1 - cross_i * g2) / (
            diagonal * delay_diag - cross_r * cross_r - cross_i * cross_i
        )
        step_u = (g1 - cross_r * step_d) / diagonal
        step_w = (g2 - cross_i * step_d) / diagonal
        gains = (u + step_u, w + step_w, tau + step_d)

        rows = jnp.concatenate(
            list(gains) + [jnp.zeros((10, stations), jnp.float32)], axis=0
        )
        got = jnp.dot(split3(rows), onehot[...], preferred_element_type=jnp.float32)
        gathered[...] = got[0:16] + got[16:32] + got[32:48]

    for n in range(3):
        gains_out[n, :, 0, :] = gains[n]

    for k in range(2):
        sin_d, cos_d, sin_c, cos_c = delay_tables(k)
        ui, wi = own_gain(0), own_gain(2)
        uj, wj = gathered[pl.ds(k, 1), own_second], gathered[pl.ds(2 + k, 1), own_second]
        g_r = ui * uj + wi * wj
        g_i = wi * uj - ui * wj
        e_r = g_r * cos_c - g_i * sin_c
        e_i = g_r * sin_c + g_i * cos_c
        for d in range(half):
            cd, sd = cos_d[d : d + 1, :], sin_d[d : d + 1, :]
            c_r, c_i, s_r, s_i = e_r * cd, e_i * cd, e_r * sd, e_i * sd
            up = pl.ds(8 * (half + d), 8)
            down = pl.ds(8 * (half - 1 - d), 8)
            for span, f_r, f_i in (
                (up, c_r - s_i, c_i + s_r),
                (down, c_r + s_i, c_i - s_r),
            ):
                m_r, m_i = model[k, 0, span, :], model[k, 1, span, :]
                res_out[k, 0, 0, span, :] = vbuf[k, 0, span, :] - (f_r * m_r - f_i * m_i)
                res_out[k, 1, 0, span, :] = vbuf[k, 1, span, :] - (f_r * m_i + f_i * m_r)


def shards(
    stations, visibility, uv_coords, source_lm, source_flux, avg_factor, station_pairs, slot_owner
):
    ch_count = lax.axis_size("ch")
    bl_count = lax.axis_size("bl")
    pol_count = lax.axis_size("pol")
    slots, chan_local = visibility.shape[2], visibility.shape[3]
    chans = chan_local * ch_count
    sources = source_lm.shape[1]
    half = chans // 16
    group = bl_count * pol_count
    sizes = (ch_count, bl_count, pol_count, slots, chan_local, chans, sources, stations)
    f32 = jnp.float32
    vmem = pl.BlockSpec(memory_space=pltpu.VMEM)
    smem = pl.BlockSpec(memory_space=pltpu.SMEM)
    dma = pltpu.SemaphoreType.DMA
    return pl.pallas_call(
        functools.partial(kernel, sizes),
        out_shape=(
            jax.ShapeDtypeStruct((2, 2, 1, chans, LANES), f32),
            jax.ShapeDtypeStruct((3, 2, 1, stations), f32),
        ),
        in_specs=[vmem, vmem, smem, smem, vmem, vmem, smem],
        out_specs=(vmem, vmem),
        scratch_shapes=[
            pltpu.VMEM((2, 2, chans, LANES), f32),
            pltpu.VMEM((ch_count - 1, 2, 2, chan_local, LANES), f32),
            pltpu.VMEM((2, 2, chans, LANES), f32),
            pltpu.VMEM((slots * sources, LANES), f32),
            pltpu.VMEM((2, 2, slots * sources * 8, LANES), f32),
            pltpu.VMEM((half, 2, slots * sources, LANES), f32),
            pltpu.VMEM((2, 4, half * 8, LANES), f32),
            pltpu.VMEM((8, LANES), jnp.int32),
            pltpu.VMEM((bl_count, 8, LANES), jnp.int32),
            pltpu.VMEM((group, 8, LANES), f32),
            pltpu.VMEM((ITERS, group, 8, LANES), f32),
            pltpu.VMEM((stations, 2 * bl_count * LANES), jnp.bfloat16),
            pltpu.VMEM((16, 2 * bl_count * LANES), f32),
            pltpu.VMEM((16, 2 * bl_count * LANES), f32),
            dma((ch_count - 1,)),
            dma((ch_count - 1,)),
            dma((bl_count - 1,)),
            dma((bl_count - 1,)),
            dma((group - 1,)),
            dma((group - 1,)),
            dma((ITERS, group - 1)),
            dma((ITERS, group - 1)),
        ],
        compiler_params=pltpu.CompilerParams(
            collective_id=0, has_side_effects=True, vmem_limit_bytes=56 * 1024 * 1024
        ),
    )(
        visibility,
        uv_coords,
        source_lm,
        source_flux,
        avg_factor.reshape(1, -1),
        station_pairs,
        slot_owner,
    )


def solution(mesh):
    placed = (
        P("pol", None, None, "ch", ("grp", "bl")),
        P(None, None, ("grp", "bl")),
        P(),
        P("pol", None),
        P(("grp", "bl")),
        P(None, ("grp", "bl")),
        P(),
    )
    return jax.shard_map(
        functools.partial(shards, 512),
        mesh=mesh,
        in_specs=placed,
        out_specs=(P("pol", None, "ch", None, ("grp", "bl")), P(None, None, "ch", "grp")),
        check_vma=False,
    )
```

```python
import functools

import jax
import jax.numpy as jnp
from jax import lax
from jax.experimental import pallas as pl
from jax.experimental.pallas import tpu as pltpu
from jax.sharding import PartitionSpec as P

ITERS = 3
LANES = 128
TILE = 4
damping = 1.0
two_pi = 6.283185307179586
MESH = pl.DeviceIdType.MESH

SIN_COEF = (
    3.141592653589793,
    -5.16771278004997,
    2.550164039877345,
    -0.5992645293207921,
    0.08214588661112823,
    -0.00737043094571435,
)
COS_COEF = (
    1.0,
    -4.934802200544679,
    4.058712126416768,
    -1.3352627688545893,
    0.2353306303588935,
    -0.02580689139001406,
    0.0019295743094039231,
)


def sincos_turns(turns):
    part = turns - jnp.floor(turns + 0.5)
    sq = part * part
    sin_half = jnp.full_like(sq, SIN_COEF[-1])
    for coef in SIN_COEF[-2::-1]:
        sin_half = sin_half * sq + coef
    sin_half = sin_half * part
    cos_half = jnp.full_like(sq, COS_COEF[-1])
    for coef in COS_COEF[-2::-1]:
        cos_half = cos_half * sq + coef
    twice = sin_half + sin_half
    return twice * cos_half, 1.0 - twice * sin_half


def split3(value):
    high = value.astype(jnp.bfloat16)
    rest = value - high.astype(jnp.float32)
    mid = rest.astype(jnp.bfloat16)
    low = (rest - mid.astype(jnp.float32)).astype(jnp.bfloat16)
    return jnp.concatenate([high, mid, low], axis=0)


def kernel(
    sizes,
    vis,
    uv,
    lm,
    flux,
    factor,
    pairs,
    owner,
    res_out,
    gains_out,
    vbuf,
    sbuf,
    model,
    geo,
    ftab,
    dtab,
    xtab,
    psend,
    pall,
    mall,
    yall,
    onehot,
    terms,
    gathered,
    trig,
    v_send,
    v_recv,
    p_send,
    p_recv,
    m_send,
    m_recv,
    y_send,
    y_recv,
):
    ch_count, bl_count, pol_count, slots, chan_local, chans, sources, stations = sizes
    ch = lax.axis_index("ch")
    bl = lax.axis_index("bl")
    pol = lax.axis_index("pol")
    group = bl_count * pol_count
    me = bl * pol_count + pol
    half = chans // 16
    base_all = bl_count * LANES

    def ch_peer(step):
        return lax.rem(ch + step, ch_count)

    def group_peer(step):
        other = lax.rem(me + step, group)
        return {"bl": other // pol_count, "pol": lax.rem(other, pol_count)}

    barrier = pltpu.get_barrier_semaphore()
    for step in range(1, ch_count):
        pl.semaphore_signal(
            barrier, inc=1, device_id={"ch": ch_peer(step)}, device_id_type=MESH
        )
    for step in range(1, group):
        pl.semaphore_signal(barrier, inc=1, device_id=group_peer(step), device_id_type=MESH)

    fac = factor[...]
    inverse = jnp.zeros(fac.shape, jnp.float32)
    power = 1
    while power <= slots:
        inverse = jnp.where(fac == power, jnp.float32(1.0 / power), inverse)
        power *= 2

    def weight_rows(position):
        slot = jnp.int32(0)
        for s in range(slots):
            slot = slot + jnp.where(owner[s] == position, jnp.int32(s), jnp.int32(0))
        return [
            jnp.where(jnp.bitwise_xor(slot, jnp.int32(t)) < fac, inverse, 0.0)
            for t in range(slots)
        ]

    def average(rows, put):
        def block(n, _):
            k, r = n // 2, lax.rem(n, 2)
            total = rows[0] * vis[k, r, 0]
            for t in range(1, slots):
                total = total + rows[t] * vis[k, r, t]
            put(k, r, total)
            return 0

        lax.fori_loop(0, 4, block, 0)

    for step in range(1, ch_count):

        def put_away(k, r, value, step=step):
            sbuf[step - 1, k, r] = value

        average(weight_rows(ch_peer(step)), put_away)
    own_rows = weight_rows(ch)
    own_span = pl.ds(pl.multiple_of(ch * chan_local, 8), chan_local)
    for i in range(2):
        psend[pl.ds(i, 1), :] = pairs[pl.ds(i, 1), :]
    psend[pl.ds(2, 6), :] = jnp.zeros((6, LANES), jnp.int32)

    pl.semaphore_wait(barrier, ch_count - 1 + group - 1)

    v_copies = []
    for step in range(1, ch_count):
        copy = pltpu.make_async_remote_copy(
            src_ref=sbuf.at[step - 1],
            dst_ref=vbuf.at[:, :, own_span, :],
            send_sem=v_send.at[step - 1],
            recv_sem=v_recv.at[step - 1],
            device_id={"ch": ch_peer(step)},
            device_id_type=MESH,
        )
        copy.start()
        v_copies.append(copy)
    p_copies = []
    for step in range(1, bl_count):
        copy = pltpu.make_async_remote_copy(
            src_ref=psend,
            dst_ref=pall.at[bl],
            send_sem=p_send.at[step - 1],
            recv_sem=p_recv.at[step - 1],
            device_id={"bl": lax.rem(bl + step, bl_count)},
            device_id_type=MESH,
        )
        copy.start()
        p_copies.append(copy)
    pall[bl] = psend[...]

    def put_own(k, r, value):
        vbuf[k, r, own_span, :] = value

    average(own_rows, put_own)

    def geo_row(s, _):
        for t in range(slots):
            geo[pl.ds(t * sources + s, 1), :] = -(
                lm[0, s] * uv[0, pl.ds(t, 1), :] + lm[1, s] * uv[1, pl.ds(t, 1), :]
            )
        return 0

    lax.fori_loop(0, sources, geo_row, 0, unroll=8)

    def offset_rows(block, _):
        span = pl.ds(pl.multiple_of(block * 32, 32), 32)
        sin_h, cos_h = sincos_turns(geo[span, :] * jnp.float32(4.0 / chans))
        cos_f = cos_h * cos_h - sin_h * sin_h
        sin_f = 2.0 * sin_h * cos_h
        for d in range(half):
            dtab[d, 0, span, :] = cos_h
            dtab[d, 1, span, :] = sin_h
            cos_h, sin_h = cos_h * cos_f - sin_h * sin_f, sin_h * cos_f + cos_h * sin_f
        return 0

    lax.fori_loop(0, slots * sources // 32, offset_rows, 0)

    sub = lax.broadcasted_iota(jnp.int32, (8, LANES), 0).astype(jnp.float32)
    freq_c = 0.5 + (sub + jnp.float32(4 * (chans // 8 - 1) + 0.5)) / chans
    omega_c = two_pi * freq_c
    omega_step = jnp.float32(two_pi * 8.0 / chans)

    for t in range(slots):
        wide = jnp.broadcast_to(own_rows[t], (8, LANES))

        def centre(s, _, t=t, wide=wide):
            row = t * sources + s
            sin_c, cos_c = sincos_turns(geo[pl.ds(row, 1), :] * freq_c)
            sin_c = sin_c * wide
            cos_c = cos_c * wide
            span = pl.ds(pl.multiple_of(row * 8, 8), 8)
            for k in range(2):
                ftab[k, 0, span, :] = flux[k, s] * cos_c
                ftab[k, 1, span, :] = flux[k, s] * sin_c
            return 0

        lax.fori_loop(0, sources, centre, 0, unroll=4)

    zero = jnp.zeros((8, LANES), jnp.float32)

    def channel_rows(d):
        up = pl.ds(pl.multiple_of(8 * (half + d), 8), 8)
        down = pl.ds(pl.multiple_of(8 * (half - 1 - d), 8), 8)
        return up, down

    def sky_tile(tile, moments):
        first = tile * TILE
        moments = list(moments)

        def add_source(row, acc):
            span = pl.ds(pl.multiple_of(row * 8, 8), 8)
            fc = [ftab[k, 0, span, :] for k in range(2)]
            fs = [ftab[k, 1, span, :] for k in range(2)]
            out = []
            at = 0
            for d in range(TILE):
                cd = jnp.broadcast_to(dtab[first + d, 0, pl.ds(row, 1), :], (8, LANES))
                sd = jnp.broadcast_to(dtab[first + d, 1, pl.ds(row, 1), :], (8, LANES))
                for k in range(2):
                    out.append(acc[at] + fc[k] * cd)
                    out.append(acc[at + 1] + fs[k] * sd)
                    out.append(acc[at + 2] + fs[k] * cd)
                    out.append(acc[at + 3] + fc[k] * sd)
                    at += 4
            return tuple(out)

        acc = lax.fori_loop(0, slots * sources, add_source, (zero,) * (8 * TILE), unroll=4)
        for d in range(TILE):
            dist = (first + d).astype(jnp.float32) + 0.5
            up, down = channel_rows(first + d)
            for k in range(2):
                cc, ss, sc, cs = acc[(d * 2 + k) * 4 : (d * 2 + k) * 4 + 4]
                up_r, up_i, dn_r, dn_i = cc - ss, sc + cs, cc + ss, sc - cs
                model[k, 0, up, :] = up_r
                model[k, 1, up, :] = up_i
                model[k, 0, down, :] = dn_r
                model[k, 1, down, :] = dn_i
                up_p = up_r * up_r + up_i * up_i
                dn_p = dn_r * dn_r + dn_i * dn_i
                both = up_p + dn_p
                moments[3 * k] = moments[3 * k] + both
                moments[3 * k + 1] = moments[3 * k + 1] + dist * (up_p - dn_p)
                moments[3 * k + 2] = moments[3 * k + 2] + (dist * dist) * both
        return tuple(moments)

    moments = lax.fori_loop(0, half // TILE, sky_tile, (zero,) * 6)

    def fold(value):
        return jnp.sum(value, axis=0, keepdims=True)

    for k in range(2):
        a0, a1, a2 = moments[3 * k : 3 * k + 3]
        mall[me, pl.ds(k, 1), :] = fold(a0)
        mall[me, pl.ds(2 + k, 1), :] = fold(omega_c * a0 + omega_step * a1)
        mall[me, pl.ds(4 + k, 1), :] = fold(
            omega_c * omega_c * a0
            + 2.0 * omega_step * omega_c * a1
            + omega_step * omega_step * a2
        )
    mall[me, pl.ds(6, 2), :] = jnp.zeros((2, LANES), jnp.float32)

    def spread(block, send_sem, recv_sem):
        copies = []
        for step in range(1, group):
            copy = pltpu.make_async_remote_copy(
                src_ref=block,
                dst_ref=block,
                send_sem=send_sem.at[step - 1],
                recv_sem=recv_sem.at[step - 1],
                device_id=group_peer(step),
                device_id_type=MESH,
            )
            copy.start()
            copies.append(copy)
        return copies

    m_copies = spread(mall.at[me], m_send, m_recv)

    for copy in p_copies:
        copy.wait()
    station = lax.broadcasted_iota(jnp.int32, (stations, LANES), 0)

    def hot_block(b, _):
        for i in range(2):
            hot = (station == pall[b, pl.ds(i, 1), :]).astype(jnp.float32)
            lanes = pl.ds(pl.multiple_of(i * base_all + b * LANES, LANES), LANES)
            onehot[:, lanes] = hot.astype(jnp.bfloat16)
        return 0

    lax.fori_loop(0, bl_count, hot_block, 0)

    for copy in v_copies:
        copy.wait()

    def product_rows(d, _):
        at = pl.ds(pl.multiple_of(8 * d, 8), 8)
        for k in range(2):
            halves = []
            for span in channel_rows(d):
                m_r, m_i = model[k, 0, span, :], model[k, 1, span, :]
                v_r, v_i = vbuf[k, 0, span, :], vbuf[k, 1, span, :]
                halves.append((m_r * v_r + m_i * v_i, m_r * v_i - m_i * v_r))
            (u_r, u_i), (l_r, l_i) = halves
            xtab[k, 0, at, :] = u_r + l_r
            xtab[k, 1, at, :] = u_i + l_i
            xtab[k, 2, at, :] = u_r - l_r
            xtab[k, 3, at, :] = u_i - l_i
        return 0

    lax.fori_loop(0, half, product_rows, 0, unroll=2)

    own_first = pl.ds(pl.multiple_of(bl * LANES, LANES), LANES)
    own_second = pl.ds(pl.multiple_of(base_all + bl * LANES, LANES), LANES)
    dist_col = lax.broadcasted_iota(jnp.int32, (half, LANES), 0).astype(jnp.float32) + 0.5

    def own_gain(row):
        return jnp.where(
            pol == 0,
            gathered[pl.ds(row, 1), own_first],
            gathered[pl.ds(row + 1, 1), own_first],
        )

    def delay_tables(k):
        tau = own_gain(4) - gathered[pl.ds(4 + k, 1), own_second]
        sin_d, cos_d = sincos_turns(dist_col * (tau * jnp.float32(8.0 / chans)))
        trig[k, 0] = cos_d
        trig[k, 1] = sin_d
        return sincos_turns(freq_c * tau)

    def offset_pair(k, d):
        cd = jnp.broadcast_to(trig[k, 0, pl.ds(d, 1), :], (8, LANES))
        sd = jnp.broadcast_to(trig[k, 1, pl.ds(d, 1), :], (8, LANES))
        return cd, sd

    gains = (
        jnp.ones((2, stations), jnp.float32),
        jnp.zeros((2, stations), jnp.float32),
        jnp.zeros((2, stations), jnp.float32),
    )
    gathered[pl.ds(0, 2), :] = jnp.ones((2, 2 * base_all), jnp.float32)
    gathered[pl.ds(2, 14), :] = jnp.zeros((14, 2 * base_all), jnp.float32)
    terms[pl.ds(12, 4), :] = jnp.zeros((4, 2 * base_all), jnp.float32)

    for copy in m_copies:
        copy.wait()

    def newton_step(it, gains):
        centres = [delay_tables(k) for k in range(2)]

        def add_offset(d, acc):
            at = pl.ds(pl.multiple_of(8 * d, 8), 8)
            dist = d.astype(jnp.float32) + 0.5
            out = []
            for k in range(2):
                u_r, u_i, w_r, w_i = acc[4 * k : 4 * k + 4]
                p_r, p_i = xtab[k, 0, at, :], xtab[k, 1, at, :]
                m_r, m_i = xtab[k, 2, at, :], xtab[k, 3, at, :]
                cd, sd = offset_pair(k, d)
                u_r = u_r + (cd * p_r + sd * m_i)
                u_i = u_i + (cd * p_i - sd * m_r)
                cd, sd = dist * cd, dist * sd
                w_r = w_r + (cd * m_r + sd * p_i)
                w_i = w_i + (cd * m_i - sd * p_r)
                out += [u_r, u_i, w_r, w_i]
            return tuple(out)

        acc = lax.fori_loop(0, half, add_offset, (zero,) * 8, unroll=4)
        for k in range(2):
            u_r, u_i, w_r, w_i = acc[4 * k : 4 * k + 4]
            sin_c, cos_c = centres[k]
            w_r = omega_c * u_r + omega_step * w_r
            w_i = omega_c * u_i + omega_step * w_i
            u_r, u_i = cos_c * u_r + sin_c * u_i, cos_c * u_i - sin_c * u_r
            w_r, w_i = cos_c * w_r + sin_c * w_i, cos_c * w_i - sin_c * w_r
            for n, value in enumerate((u_r, u_i, w_r, w_i)):
                yall[it, me, pl.ds(2 * n + k, 1), :] = fold(value)
        for copy in spread(yall.at[it, me], y_send.at[it], y_recv.at[it]):
            copy.wait()

        def term_block(b, _):
            lane_1 = pl.ds(pl.multiple_of(b * LANES, LANES), LANES)
            lane_2 = pl.ds(pl.multiple_of(base_all + b * LANES, LANES), LANES)
            uj, wj = gathered[pl.ds(0, 2), lane_2], gathered[pl.ds(2, 2), lane_2]
            nj = uj * uj + wj * wj
            second = [jnp.zeros((2, LANES), jnp.float32)] * 6
            for p in range(pol_count):
                dev = b * pol_count + p
                ui, wi = gathered[pl.ds(p, 1), lane_1], gathered[pl.ds(2 + p, 1), lane_1]
                ni = ui * ui + wi * wi
                y0r, y0i, y1r, y1i = [yall[it, dev, pl.ds(2 * n, 2), :] for n in range(4)]
                p0, p1, p2 = [mall[dev, pl.ds(2 * n, 2), :] for n in range(3)]
                b_r = uj * y1r - wj * y1i
                b_i = uj * y1i + wj * y1r
                cross = ui * b_i - wi * b_r
                s0 = nj * p0
                first = (
                    s0,
                    nj * p1,
                    nj * p2,
                    uj * y0r - wj * y0i - ui * s0,
                    uj * y0i + wj * y0r - wi * s0,
                    cross,
                )
                for x in range(6):
                    terms[pl.ds(2 * x + p, 1), lane_1] = fold(first[x])
                t0 = ni * p0
                more = (
                    t0,
                    ni * p1,
                    ni * p2,
                    ui * y0r + wi * y0i - uj * t0,
                    -(ui * y0i - wi * y0r + wj * t0),
                    -cross,
                )
                second = [a + c for a, c in zip(second, more)]
            for x in range(6):
                terms[pl.ds(2 * x, 2), lane_2] = second[x]
            return 0

        lax.fori_loop(0, bl_count, term_block, 0, unroll=2)

        summed = lax.dot_general(
            split3(terms[...]),
            onehot[...],
            (((1,), (1,)), ((), ())),
            preferred_element_type=jnp.float32,
        )
        summed = summed[0:16] + summed[16:32] + summed[32:48]
        s0, s1, s2, g1, g2, g3 = [summed[2 * x : 2 * x + 2] for x in range(6)]
        u, w, tau = gains
        diagonal = (1.0 + damping) * s0 + 1.0
        cross_r = -w * s1
        cross_i = u * s1
        delay_diag = (1.0 + damping) * (u * u + w * w) * s2 + 1.0
        step_d = (diagonal * g3 - cross_r * g1 - cross_i * g2) / (
            diagonal * delay_diag - cross_r * cross_r - cross_i * cross_i
        )
        step_u = (g1 - cross_r * step_d) / diagonal
        step_w = (g2 - cross_i * step_d) / diagonal
        gains = (u + step_u, w + step_w, tau + step_d)

        rows = jnp.concatenate(
            list(gains) + [jnp.zeros((10, stations), jnp.float32)], axis=0
        )
        got = jnp.dot(split3(rows), onehot[...], preferred_element_type=jnp.float32)
        gathered[...] = got[0:16] + got[16:32] + got[32:48]
        return gains

    gains = lax.fori_loop(0, ITERS, newton_step, gains)

    for n in range(3):
        gains_out[n, :, 0, :] = gains[n]

    for k in range(2):
        sin_c, cos_c = delay_tables(k)
        ui, wi = own_gain(0), own_gain(2)
        uj, wj = gathered[pl.ds(k, 1), own_second], gathered[pl.ds(2 + k, 1), own_second]
        g_r = ui * uj + wi * wj
        g_i = wi * uj - ui * wj
        e_r = g_r * cos_c - g_i * sin_c
        e_i = g_r * sin_c + g_i * cos_c

        def residual_rows(d, _, k=k, e_r=e_r, e_i=e_i):
            cd, sd = offset_pair(k, d)
            c_r, c_i, s_r, s_i = e_r * cd, e_i * cd, e_r * sd, e_i * sd
            up, down = channel_rows(d)
            for span, f_r, f_i in (
                (up, c_r - s_i, c_i + s_r),
                (down, c_r + s_i, c_i - s_r),
            ):
                m_r, m_i = model[k, 0, span, :], model[k, 1, span, :]
                res_out[k, 0, 0, span, :] = vbuf[k, 0, span, :] - (f_r * m_r - f_i * m_i)
                res_out[k, 1, 0, span, :] = vbuf[k, 1, span, :] - (f_r * m_i + f_i * m_r)
            return 0

        lax.fori_loop(0, half, residual_rows, 0, unroll=4)


def shards(
    stations, visibility, uv_coords, source_lm, source_flux, avg_factor, station_pairs, slot_owner
):
    ch_count = lax.axis_size("ch")
    bl_count = lax.axis_size("bl")
    pol_count = lax.axis_size("pol")
    slots, chan_local = visibility.shape[2], visibility.shape[3]
    chans = chan_local * ch_count
    sources = source_lm.shape[1]
    half = chans // 16
    group = bl_count * pol_count
    sizes = (ch_count, bl_count, pol_count, slots, chan_local, chans, sources, stations)
    f32 = jnp.float32
    vmem = pl.BlockSpec(memory_space=pltpu.VMEM)
    smem = pl.BlockSpec(memory_space=pltpu.SMEM)
    dma = pltpu.SemaphoreType.DMA
    return pl.pallas_call(
        functools.partial(kernel, sizes),
        out_shape=(
            jax.ShapeDtypeStruct((2, 2, 1, chans, LANES), f32),
            jax.ShapeDtypeStruct((3, 2, 1, stations), f32),
        ),
        in_specs=[vmem, vmem, smem, smem, vmem, vmem, smem],
        out_specs=(vmem, vmem),
        scratch_shapes=[
            pltpu.VMEM((2, 2, chans, LANES), f32),
            pltpu.VMEM((ch_count - 1, 2, 2, chan_local, LANES), f32),
            pltpu.VMEM((2, 2, chans, LANES), f32),
            pltpu.VMEM((slots * sources, LANES), f32),
            pltpu.VMEM((2, 2, slots * sources * 8, LANES), f32),
            pltpu.VMEM((half, 2, slots * sources, LANES), f32),
            pltpu.VMEM((2, 4, half * 8, LANES), f32),
            pltpu.VMEM((8, LANES), jnp.int32),
            pltpu.VMEM((bl_count, 8, LANES), jnp.int32),
            pltpu.VMEM((group, 8, LANES), f32),
            pltpu.VMEM((ITERS, group, 8, LANES), f32),
            pltpu.VMEM((stations, 2 * bl_count * LANES), jnp.bfloat16),
            pltpu.VMEM((16, 2 * bl_count * LANES), f32),
            pltpu.VMEM((16, 2 * bl_count * LANES), f32),
            pltpu.VMEM((2, 2, half, LANES), f32),
            dma((ch_count - 1,)),
            dma((ch_count - 1,)),
            dma((bl_count - 1,)),
            dma((bl_count - 1,)),
            dma((group - 1,)),
            dma((group - 1,)),
            dma((ITERS, group - 1)),
            dma((ITERS, group - 1)),
        ],
        compiler_params=pltpu.CompilerParams(
            collective_id=0, has_side_effects=True, vmem_limit_bytes=56 * 1024 * 1024
        ),
    )(
        visibility,
        uv_coords,
        source_lm,
        source_flux,
        avg_factor.reshape(1, -1),
        station_pairs,
        slot_owner,
    )


def solution(mesh):
    placed = (
        P("pol", None, None, "ch", ("grp", "bl")),
        P(None, None, ("grp", "bl")),
        P(),
        P("pol", None),
        P(("grp", "bl")),
        P(None, ("grp", "bl")),
        P(),
    )
    return jax.shard_map(
        functools.partial(shards, 512),
        mesh=mesh,
        in_specs=placed,
        out_specs=(P("pol", None, "ch", None, ("grp", "bl")), P(None, None, "ch", "grp")),
        check_vma=False,
    )
```

```python
import functools

import jax
import jax.numpy as jnp
from jax import lax
from jax.experimental import pallas as pl
from jax.experimental.pallas import tpu as pltpu
from jax.sharding import PartitionSpec as P

ITERS = 3
LANES = 128
TILE = 4
damping = 1.0
two_pi = 6.283185307179586
MESH = pl.DeviceIdType.MESH

SIN_COEF = (
    3.141592653589793,
    -5.16771278004997,
    2.550164039877345,
    -0.5992645293207921,
    0.08214588661112823,
    -0.00737043094571435,
)
COS_COEF = (
    1.0,
    -4.934802200544679,
    4.058712126416768,
    -1.3352627688545893,
    0.2353306303588935,
    -0.02580689139001406,
    0.0019295743094039231,
)


def sincos_turns(turns):
    part = turns - jnp.floor(turns + 0.5)
    sq = part * part
    sin_half = jnp.full_like(sq, SIN_COEF[-1])
    for coef in SIN_COEF[-2::-1]:
        sin_half = sin_half * sq + coef
    sin_half = sin_half * part
    cos_half = jnp.full_like(sq, COS_COEF[-1])
    for coef in COS_COEF[-2::-1]:
        cos_half = cos_half * sq + coef
    twice = sin_half + sin_half
    return twice * cos_half, 1.0 - twice * sin_half


def split3(value):
    high = value.astype(jnp.bfloat16)
    rest = value - high.astype(jnp.float32)
    mid = rest.astype(jnp.bfloat16)
    low = (rest - mid.astype(jnp.float32)).astype(jnp.bfloat16)
    return jnp.concatenate([high, mid, low], axis=0)


def kernel(
    sizes,
    vis_hbm,
    uv,
    lm,
    flux,
    factor,
    pairs,
    owner,
    res_out,
    gains_out,
    vbuf,
    sbuf,
    model,
    geo,
    ftab,
    dtab,
    xtab,
    psend,
    pall,
    mall,
    yall,
    onehot,
    terms,
    gathered,
    v_send,
    v_recv,
    p_send,
    p_recv,
    m_send,
    m_recv,
    y_send,
    y_recv,
    vis,
    vis_sem,
):
    ch_count, bl_count, pol_count, slots, chan_local, chans, sources, stations = sizes
    ch = lax.axis_index("ch")
    bl = lax.axis_index("bl")
    pol = lax.axis_index("pol")
    group = bl_count * pol_count
    me = bl * pol_count + pol
    half = chans // 16
    base_all = bl_count * LANES

    def ch_peer(step):
        return lax.rem(ch + step, ch_count)

    def group_peer(step):
        other = lax.rem(me + step, group)
        return {"bl": other // pol_count, "pol": lax.rem(other, pol_count)}

    load = pltpu.make_async_copy(vis_hbm, vis, vis_sem)
    load.start()
    barrier = pltpu.get_barrier_semaphore()
    for step in range(1, ch_count):
        pl.semaphore_signal(
            barrier, inc=1, device_id={"ch": ch_peer(step)}, device_id_type=MESH
        )
    for step in range(1, group):
        pl.semaphore_signal(barrier, inc=1, device_id=group_peer(step), device_id_type=MESH)

    fac = factor[...]
    inverse = jnp.zeros(fac.shape, jnp.float32)
    power = 1
    while power <= slots:
        inverse = jnp.where(fac == power, jnp.float32(1.0 / power), inverse)
        power *= 2

    def weight_rows(position):
        slot = jnp.int32(0)
        for s in range(slots):
            slot = slot + jnp.where(owner[s] == position, jnp.int32(s), jnp.int32(0))
        return [
            jnp.where(jnp.bitwise_xor(slot, jnp.int32(t)) < fac, inverse, 0.0)
            for t in range(slots)
        ]

    def averaged(rows, k, r):
        total = rows[0] * vis[k, r, 0]
        for t in range(1, slots):
            total = total + rows[t] * vis[k, r, t]
        return total

    own_rows = weight_rows(ch)
    own_span = pl.ds(pl.multiple_of(ch * chan_local, 8), chan_local)
    for i in range(2):
        psend[pl.ds(i, 1), :] = pairs[pl.ds(i, 1), :]
    psend[pl.ds(2, 6), :] = jnp.zeros((6, LANES), jnp.int32)

    def geo_row(s, _):
        for t in range(slots):
            geo[pl.ds(t * sources + s, 1), :] = -(
                lm[0, s] * uv[0, pl.ds(t, 1), :] + lm[1, s] * uv[1, pl.ds(t, 1), :]
            )
        return 0

    lax.fori_loop(0, sources, geo_row, 0, unroll=8)

    def offset_rows(block, _):
        span = pl.ds(pl.multiple_of(block * 32, 32), 32)
        sin_h, cos_h = sincos_turns(geo[span, :] * jnp.float32(4.0 / chans))
        cos_f = cos_h * cos_h - sin_h * sin_h
        sin_f = 2.0 * sin_h * cos_h
        for d in range(half):
            dtab[d, 0, span, :] = cos_h
            dtab[d, 1, span, :] = sin_h
            cos_h, sin_h = cos_h * cos_f - sin_h * sin_f, sin_h * cos_f + cos_h * sin_f
        return 0

    lax.fori_loop(0, slots * sources // 32, offset_rows, 0)

    sub = lax.broadcasted_iota(jnp.int32, (8, LANES), 0).astype(jnp.float32)
    freq_c = 0.5 + (sub + jnp.float32(4 * (chans // 8 - 1) + 0.5)) / chans
    omega_c = two_pi * freq_c
    omega_step = jnp.float32(two_pi * 8.0 / chans)

    for t in range(slots):
        wide = jnp.broadcast_to(own_rows[t], (8, LANES))

        def centre(s, _, t=t, wide=wide):
            row = t * sources + s
            sin_c, cos_c = sincos_turns(geo[pl.ds(row, 1), :] * freq_c)
            sin_c = sin_c * wide
            cos_c = cos_c * wide
            span = pl.ds(pl.multiple_of(row * 8, 8), 8)
            for k in range(2):
                ftab[k, 0, span, :] = flux[k, s] * cos_c
                ftab[k, 1, span, :] = flux[k, s] * sin_c
            return 0

        lax.fori_loop(0, sources, centre, 0, unroll=4)

    load.wait()
    for step in range(1, ch_count):
        rows = weight_rows(ch_peer(step))
        for k in range(2):
            for r in range(2):
                sbuf[step - 1, k, r] = averaged(rows, k, r)
    pl.semaphore_wait(barrier, ch_count - 1 + group - 1)

    v_copies = []
    for step in range(1, ch_count):
        copy = pltpu.make_async_remote_copy(
            src_ref=sbuf.at[step - 1],
            dst_ref=vbuf.at[:, :, own_span, :],
            send_sem=v_send.at[step - 1],
            recv_sem=v_recv.at[step - 1],
            device_id={"ch": ch_peer(step)},
            device_id_type=MESH,
        )
        copy.start()
        v_copies.append(copy)
    p_copies = []
    for step in range(1, bl_count):
        copy = pltpu.make_async_remote_copy(
            src_ref=psend,
            dst_ref=pall.at[bl],
            send_sem=p_send.at[step - 1],
            recv_sem=p_recv.at[step - 1],
            device_id={"bl": lax.rem(bl + step, bl_count)},
            device_id_type=MESH,
        )
        copy.start()
        p_copies.append(copy)
    pall[bl] = psend[...]
    for k in range(2):
        for r in range(2):
            vbuf[k, r, own_span, :] = averaged(own_rows, k, r)

    zero = jnp.zeros((8, LANES), jnp.float32)
    moments = [[zero, zero, zero] for _ in range(2)]
    for first in range(0, half, TILE):
        count = min(TILE, half - first)

        def add_source(row, acc, first=first, count=count):
            span = pl.ds(pl.multiple_of(row * 8, 8), 8)
            fc = [ftab[k, 0, span, :] for k in range(2)]
            fs = [ftab[k, 1, span, :] for k in range(2)]
            out = []
            at = 0
            for d in range(count):
                cd = jnp.broadcast_to(dtab[first + d, 0, pl.ds(row, 1), :], (8, LANES))
                sd = jnp.broadcast_to(dtab[first + d, 1, pl.ds(row, 1), :], (8, LANES))
                for k in range(2):
                    out.append(acc[at] + fc[k] * cd)
                    out.append(acc[at + 1] + fs[k] * sd)
                    out.append(acc[at + 2] + fs[k] * cd)
                    out.append(acc[at + 3] + fc[k] * sd)
                    at += 4
            return tuple(out)

        acc = lax.fori_loop(
            0, slots * sources, add_source, (zero,) * (8 * count), unroll=4
        )
        for d in range(count):
            dist = jnp.float32(first + d + 0.5)
            up = pl.ds(8 * (half + first + d), 8)
            down = pl.ds(8 * (half - 1 - first - d), 8)
            for k in range(2):
                cc, ss, sc, cs = acc[(d * 2 + k) * 4 : (d * 2 + k) * 4 + 4]
                up_r, up_i, dn_r, dn_i = cc - ss, sc + cs, cc + ss, sc - cs
                model[k, 0, up, :] = up_r
                model[k, 1, up, :] = up_i
                model[k, 0, down, :] = dn_r
                model[k, 1, down, :] = dn_i
                up_p = up_r * up_r + up_i * up_i
                dn_p = dn_r * dn_r + dn_i * dn_i
                both = up_p + dn_p
                moments[k][0] = moments[k][0] + both
                moments[k][1] = moments[k][1] + dist * (up_p - dn_p)
                moments[k][2] = moments[k][2] + (dist * dist) * both

    def fold(value):
        return jnp.sum(value, axis=0, keepdims=True)

    for k in range(2):
        a0, a1, a2 = moments[k]
        mall[me, pl.ds(k, 1), :] = fold(a0)
        mall[me, pl.ds(2 + k, 1), :] = fold(omega_c * a0 + omega_step * a1)
        mall[me, pl.ds(4 + k, 1), :] = fold(
            omega_c * omega_c * a0
            + 2.0 * omega_step * omega_c * a1
            + omega_step * omega_step * a2
        )
    mall[me, pl.ds(6, 2), :] = jnp.zeros((2, LANES), jnp.float32)

    def spread(block, send_sem, recv_sem):
        copies = []
        for step in range(1, group):
            copy = pltpu.make_async_remote_copy(
                src_ref=block,
                dst_ref=block,
                send_sem=send_sem.at[step - 1],
                recv_sem=recv_sem.at[step - 1],
                device_id=group_peer(step),
                device_id_type=MESH,
            )
            copy.start()
            copies.append(copy)
        return copies

    m_copies = spread(mall.at[me], m_send, m_recv)

    for copy in p_copies:
        copy.wait()
    station = lax.broadcasted_iota(jnp.int32, (stations, LANES), 0)
    for b in range(bl_count):
        for i in range(2):
            hot = (station == pall[b, pl.ds(i, 1), :]).astype(jnp.float32)
            onehot[:, pl.ds(i * base_all + b * LANES, LANES)] = hot.astype(jnp.bfloat16)

    for copy in v_copies:
        copy.wait()

    for d in range(half):
        up = pl.ds(8 * (half + d), 8)
        down = pl.ds(8 * (half - 1 - d), 8)
        at = pl.ds(8 * d, 8)
        for k in range(2):
            halves = []
            for span in (up, down):
                m_r, m_i = model[k, 0, span, :], model[k, 1, span, :]
                v_r, v_i = vbuf[k, 0, span, :], vbuf[k, 1, span, :]
                halves.append((m_r * v_r + m_i * v_i, m_r * v_i - m_i * v_r))
            (u_r, u_i), (l_r, l_i) = halves
            xtab[k, 0, at, :] = u_r + l_r
            xtab[k, 1, at, :] = u_i + l_i
            xtab[k, 2, at, :] = u_r - l_r
            xtab[k, 3, at, :] = u_i - l_i

    own_first = pl.ds(pl.multiple_of(bl * LANES, LANES), LANES)
    own_second = pl.ds(pl.multiple_of(base_all + bl * LANES, LANES), LANES)
    dist_col = lax.broadcasted_iota(jnp.int32, (half, LANES), 0).astype(jnp.float32) + 0.5

    def own_gain(row):
        return jnp.where(
            pol == 0,
            gathered[pl.ds(row, 1), own_first],
            gathered[pl.ds(row + 1, 1), own_first],
        )

    def delay_tables(k):
        tau = own_gain(4) - gathered[pl.ds(4 + k, 1), own_second]
        sin_d, cos_d = sincos_turns(dist_col * (tau * jnp.float32(8.0 / chans)))
        sin_c, cos_c = sincos_turns(freq_c * tau)
        return sin_d, cos_d, sin_c, cos_c

    gains = (
        jnp.ones((2, stations), jnp.float32),
        jnp.zeros((2, stations), jnp.float32),
        jnp.zeros((2, stations), jnp.float32),
    )
    gathered[pl.ds(0, 2), :] = jnp.ones((2, 2 * base_all), jnp.float32)
    gathered[pl.ds(2, 14), :] = jnp.zeros((14, 2 * base_all), jnp.float32)
    terms[pl.ds(12, 4), :] = jnp.zeros((4, 2 * base_all), jnp.float32)

    for it in range(ITERS):
        for k in range(2):
            if it > 0:
                sin_d, cos_d, sin_c, cos_c = delay_tables(k)
            u_r, u_i, w_r, w_i = zero, zero, zero, zero
            for d in range(half):
                at = pl.ds(8 * d, 8)
                p_r, p_i = xtab[k, 0, at, :], xtab[k, 1, at, :]
                m_r, m_i = xtab[k, 2, at, :], xtab[k, 3, at, :]
                dist = jnp.float32(d + 0.5)
                if it > 0:
                    cd, sd = cos_d[d : d + 1, :], sin_d[d : d + 1, :]
                    u_r = u_r + (cd * p_r + sd * m_i)
                    u_i = u_i + (cd * p_i - sd * m_r)
                    cd, sd = dist * cd, dist * sd
                    w_r = w_r + (cd * m_r + sd * p_i)
                    w_i = w_i + (cd * m_i - sd * p_r)
                else:
                    u_r = u_r + p_r
                    u_i = u_i + p_i
                    w_r = w_r + dist * m_r
                    w_i = w_i + dist * m_i
            w_r = omega_c * u_r + omega_step * w_r
            w_i = omega_c * u_i + omega_step * w_i
            if it > 0:
                u_r, u_i = cos_c * u_r + sin_c * u_i, cos_c * u_i - sin_c * u_r
                w_r, w_i = cos_c * w_r + sin_c * w_i, cos_c * w_i - sin_c * w_r
            for n, value in enumerate((u_r, u_i, w_r, w_i)):
                yall[it, me, pl.ds(2 * n + k, 1), :] = fold(value)
        copies = spread(yall.at[it, me], y_send.at[it], y_recv.at[it])
        if it == 0:
            for copy in m_copies:
                copy.wait()
        for copy in copies:
            copy.wait()

        for b in range(bl_count):
            lane_1 = pl.ds(b * LANES, LANES)
            lane_2 = pl.ds(base_all + b * LANES, LANES)
            uj, wj = gathered[pl.ds(0, 2), lane_2], gathered[pl.ds(2, 2), lane_2]
            nj = uj * uj + wj * wj
            second = [jnp.zeros((2, LANES), jnp.float32)] * 6
            for p in range(pol_count):
                dev = b * pol_count + p
                ui, wi = gathered[pl.ds(p, 1), lane_1], gathered[pl.ds(2 + p, 1), lane_1]
                ni = ui * ui + wi * wi
                y0r, y0i, y1r, y1i = [yall[it, dev, pl.ds(2 * n, 2), :] for n in range(4)]
                p0, p1, p2 = [mall[dev, pl.ds(2 * n, 2), :] for n in range(3)]
                b_r = uj * y1r - wj * y1i
                b_i = uj * y1i + wj * y1r
                cross = ui * b_i - wi * b_r
                s0 = nj * p0
                first = (
                    s0,
                    nj * p1,
                    nj * p2,
                    uj * y0r - wj * y0i - ui * s0,
                    uj * y0i + wj * y0r - wi * s0,
                    cross,
                )
                for x in range(6):
                    terms[pl.ds(2 * x + p, 1), lane_1] = fold(first[x])
                t0 = ni * p0
                more = (
                    t0,
                    ni * p1,
                    ni * p2,
                    ui * y0r + wi * y0i - uj * t0,
                    -(ui * y0i - wi * y0r + wj * t0),
                    -cross,
                )
                second = [a + c for a, c in zip(second, more)]
            for x in range(6):
                terms[pl.ds(2 * x, 2), lane_2] = second[x]

        summed = lax.dot_general(
            split3(terms[...]),
            onehot[...],
            (((1,), (1,)), ((), ())),
            preferred_element_type=jnp.float32,
        )
        summed = summed[0:16] + summed[16:32] + summed[32:48]
        s0, s1, s2, g1, g2, g3 = [summed[2 * x : 2 * x + 2] for x in range(6)]
        u, w, tau = gains
        diagonal = (1.0 + damping) * s0 + 1.0
        cross_r = -w * s1
        cross_i = u * s1
        delay_diag = (1.0 + damping) * (u * u + w * w) * s2 + 1.0
        step_d = (diagonal * g3 - cross_r * g1 - cross_i * g2) / (
            diagonal * delay_diag - cross_r * cross_r - cross_i * cross_i
        )
        step_u = (g1 - cross_r * step_d) / diagonal
        step_w = (g2 - cross_i * step_d) / diagonal
        gains = (u + step_u, w + step_w, tau + step_d)

        rows = jnp.concatenate(
            list(gains) + [jnp.zeros((10, stations), jnp.float32)], axis=0
        )
        got = jnp.dot(split3(rows), onehot[...], preferred_element_type=jnp.float32)
        gathered[...] = got[0:16] + got[16:32] + got[32:48]

    for n in range(3):
        gains_out[n, :, 0, :] = gains[n]

    for k in range(2):
        sin_d, cos_d, sin_c, cos_c = delay_tables(k)
        ui, wi = own_gain(0), own_gain(2)
        uj, wj = gathered[pl.ds(k, 1), own_second], gathered[pl.ds(2 + k, 1), own_second]
        g_r = ui * uj + wi * wj
        g_i = wi * uj - ui * wj
        e_r = g_r * cos_c - g_i * sin_c
        e_i = g_r * sin_c + g_i * cos_c
        for d in range(half):
            cd, sd = cos_d[d : d + 1, :], sin_d[d : d + 1, :]
            c_r, c_i, s_r, s_i = e_r * cd, e_i * cd, e_r * sd, e_i * sd
            up = pl.ds(8 * (half + d), 8)
            down = pl.ds(8 * (half - 1 - d), 8)
            for span, f_r, f_i in (
                (up, c_r - s_i, c_i + s_r),
                (down, c_r + s_i, c_i - s_r),
            ):
                m_r, m_i = model[k, 0, span, :], model[k, 1, span, :]
                res_out[k, 0, 0, span, :] = vbuf[k, 0, span, :] - (f_r * m_r - f_i * m_i)
                res_out[k, 1, 0, span, :] = vbuf[k, 1, span, :] - (f_r * m_i + f_i * m_r)


def shards(
    stations, visibility, uv_coords, source_lm, source_flux, avg_factor, station_pairs, slot_owner
):
    ch_count = lax.axis_size("ch")
    bl_count = lax.axis_size("bl")
    pol_count = lax.axis_size("pol")
    slots, chan_local = visibility.shape[2], visibility.shape[3]
    chans = chan_local * ch_count
    sources = source_lm.shape[1]
    half = chans // 16
    group = bl_count * pol_count
    sizes = (ch_count, bl_count, pol_count, slots, chan_local, chans, sources, stations)
    f32 = jnp.float32
    vmem = pl.BlockSpec(memory_space=pltpu.VMEM)
    smem = pl.BlockSpec(memory_space=pltpu.SMEM)
    dma = pltpu.SemaphoreType.DMA
    return pl.pallas_call(
        functools.partial(kernel, sizes),
        out_shape=(
            jax.ShapeDtypeStruct((2, 2, 1, chans, LANES), f32),
            jax.ShapeDtypeStruct((3, 2, 1, stations), f32),
        ),
        in_specs=[pl.BlockSpec(memory_space=pl.ANY), vmem, smem, smem, vmem, vmem, smem],
        out_specs=(vmem, vmem),
        scratch_shapes=[
            pltpu.VMEM((2, 2, chans, LANES), f32),
            pltpu.VMEM((ch_count - 1, 2, 2, chan_local, LANES), f32),
            pltpu.VMEM((2, 2, chans, LANES), f32),
            pltpu.VMEM((slots * sources, LANES), f32),
            pltpu.VMEM((2, 2, slots * sources * 8, LANES), f32),
            pltpu.VMEM((half, 2, slots * sources, LANES), f32),
            pltpu.VMEM((2, 4, half * 8, LANES), f32),
            pltpu.VMEM((8, LANES), jnp.int32),
            pltpu.VMEM((bl_count, 8, LANES), jnp.int32),
            pltpu.VMEM((group, 8, LANES), f32),
            pltpu.VMEM((ITERS, group, 8, LANES), f32),
            pltpu.VMEM((stations, 2 * bl_count * LANES), jnp.bfloat16),
            pltpu.VMEM((16, 2 * bl_count * LANES), f32),
            pltpu.VMEM((16, 2 * bl_count * LANES), f32),
            dma((ch_count - 1,)),
            dma((ch_count - 1,)),
            dma((bl_count - 1,)),
            dma((bl_count - 1,)),
            dma((group - 1,)),
            dma((group - 1,)),
            dma((ITERS, group - 1)),
            dma((ITERS, group - 1)),
            pltpu.VMEM(visibility.shape, f32),
            dma,
        ],
        compiler_params=pltpu.CompilerParams(
            collective_id=0, has_side_effects=True, vmem_limit_bytes=56 * 1024 * 1024
        ),
    )(
        visibility,
        uv_coords,
        source_lm,
        source_flux,
        avg_factor.reshape(1, -1),
        station_pairs,
        slot_owner,
    )


def solution(mesh):
    placed = (
        P("pol", None, None, "ch", ("grp", "bl")),
        P(None, None, ("grp", "bl")),
        P(),
        P("pol", None),
        P(("grp", "bl")),
        P(None, ("grp", "bl")),
        P(),
    )
    return jax.shard_map(
        functools.partial(shards, 512),
        mesh=mesh,
        in_specs=placed,
        out_specs=(P("pol", None, "ch", None, ("grp", "bl")), P(None, None, "ch", "grp")),
        check_vma=False,
    )
```

```python
import functools

import jax
import jax.numpy as jnp
from jax import lax
from jax.experimental import pallas as pl
from jax.experimental.pallas import tpu as pltpu
from jax.sharding import PartitionSpec as P

ITERS = 3
LANES = 128
TILE = 4
damping = 1.0
two_pi = 6.283185307179586
MESH = pl.DeviceIdType.MESH

SIN_COEF = (
    3.141592653589793,
    -5.16771278004997,
    2.550164039877345,
    -0.5992645293207921,
    0.08214588661112823,
    -0.00737043094571435,
)
COS_COEF = (
    1.0,
    -4.934802200544679,
    4.058712126416768,
    -1.3352627688545893,
    0.2353306303588935,
    -0.02580689139001406,
    0.0019295743094039231,
)


def sincos_turns(turns):
    part = turns - jnp.floor(turns + 0.5)
    sq = part * part
    sin_half = jnp.full_like(sq, SIN_COEF[-1])
    for coef in SIN_COEF[-2::-1]:
        sin_half = sin_half * sq + coef
    sin_half = sin_half * part
    cos_half = jnp.full_like(sq, COS_COEF[-1])
    for coef in COS_COEF[-2::-1]:
        cos_half = cos_half * sq + coef
    twice = sin_half + sin_half
    return twice * cos_half, 1.0 - twice * sin_half


def split3(value):
    high = value.astype(jnp.bfloat16)
    rest = value - high.astype(jnp.float32)
    mid = rest.astype(jnp.bfloat16)
    low = (rest - mid.astype(jnp.float32)).astype(jnp.bfloat16)
    return jnp.concatenate([high, mid, low], axis=0)


def kernel(
    sizes,
    vis_hbm,
    uv,
    lm,
    flux,
    factor,
    pairs,
    owner,
    data_out,
    model_out,
    trig_out,
    turn_out,
    gains_out,
    vbuf,
    sbuf,
    model,
    geo,
    ftab,
    dtab,
    xtab,
    psend,
    pall,
    mall,
    yall,
    onehot,
    terms,
    gathered,
    v_send,
    v_recv,
    p_send,
    p_recv,
    m_send,
    m_recv,
    y_send,
    y_recv,
    vis,
    vis_sem,
    out_sem,
):
    ch_count, bl_count, pol_count, slots, chan_local, chans, sources, stations = sizes
    ch = lax.axis_index("ch")
    bl = lax.axis_index("bl")
    pol = lax.axis_index("pol")
    group = bl_count * pol_count
    me = bl * pol_count + pol
    half = chans // 16
    base_all = bl_count * LANES

    def ch_peer(step):
        return lax.rem(ch + step, ch_count)

    def group_peer(step):
        other = lax.rem(me + step, group)
        return {"bl": other // pol_count, "pol": lax.rem(other, pol_count)}

    load = pltpu.make_async_copy(vis_hbm, vis, vis_sem)
    load.start()
    barrier = pltpu.get_barrier_semaphore()
    for step in range(1, ch_count):
        pl.semaphore_signal(
            barrier, inc=1, device_id={"ch": ch_peer(step)}, device_id_type=MESH
        )
    for step in range(1, group):
        pl.semaphore_signal(barrier, inc=1, device_id=group_peer(step), device_id_type=MESH)

    fac = factor[...]
    inverse = jnp.zeros(fac.shape, jnp.float32)
    power = 1
    while power <= slots:
        inverse = jnp.where(fac == power, jnp.float32(1.0 / power), inverse)
        power *= 2

    def weight_rows(position):
        slot = jnp.int32(0)
        for s in range(slots):
            slot = slot + jnp.where(owner[s] == position, jnp.int32(s), jnp.int32(0))
        return [
            jnp.where(jnp.bitwise_xor(slot, jnp.int32(t)) < fac, inverse, 0.0)
            for t in range(slots)
        ]

    def averaged(rows, k, r):
        total = rows[0] * vis[k, r, 0]
        for t in range(1, slots):
            total = total + rows[t] * vis[k, r, t]
        return total

    own_rows = weight_rows(ch)
    own_span = pl.ds(pl.multiple_of(ch * chan_local, 8), chan_local)
    for i in range(2):
        psend[pl.ds(i, 1), :] = pairs[pl.ds(i, 1), :]
    psend[pl.ds(2, 6), :] = jnp.zeros((6, LANES), jnp.int32)

    def geo_row(s, _):
        for t in range(slots):
            geo[pl.ds(t * sources + s, 1), :] = -(
                lm[0, s] * uv[0, pl.ds(t, 1), :] + lm[1, s] * uv[1, pl.ds(t, 1), :]
            )
        return 0

    lax.fori_loop(0, sources, geo_row, 0, unroll=8)

    def offset_rows(block, _):
        span = pl.ds(pl.multiple_of(block * 32, 32), 32)
        sin_h, cos_h = sincos_turns(geo[span, :] * jnp.float32(4.0 / chans))
        cos_f = cos_h * cos_h - sin_h * sin_h
        sin_f = 2.0 * sin_h * cos_h
        for d in range(half):
            dtab[d, 0, span, :] = cos_h
            dtab[d, 1, span, :] = sin_h
            cos_h, sin_h = cos_h * cos_f - sin_h * sin_f, sin_h * cos_f + cos_h * sin_f
        return 0

    lax.fori_loop(0, slots * sources // 32, offset_rows, 0)

    sub = lax.broadcasted_iota(jnp.int32, (8, LANES), 0).astype(jnp.float32)
    freq_c = 0.5 + (sub + jnp.float32(4 * (chans // 8 - 1) + 0.5)) / chans
    omega_c = two_pi * freq_c
    omega_step = jnp.float32(two_pi * 8.0 / chans)

    for t in range(slots):
        wide = jnp.broadcast_to(own_rows[t], (8, LANES))

        def centre(s, _, t=t, wide=wide):
            row = t * sources + s
            sin_c, cos_c = sincos_turns(geo[pl.ds(row, 1), :] * freq_c)
            sin_c = sin_c * wide
            cos_c = cos_c * wide
            span = pl.ds(pl.multiple_of(row * 8, 8), 8)
            for k in range(2):
                ftab[k, 0, span, :] = flux[k, s] * cos_c
                ftab[k, 1, span, :] = flux[k, s] * sin_c
            return 0

        lax.fori_loop(0, sources, centre, 0, unroll=4)

    load.wait()
    for step in range(1, ch_count):
        rows = weight_rows(ch_peer(step))
        for k in range(2):
            for r in range(2):
                sbuf[step - 1, k, r] = averaged(rows, k, r)
    pl.semaphore_wait(barrier, ch_count - 1 + group - 1)

    v_copies = []
    for step in range(1, ch_count):
        copy = pltpu.make_async_remote_copy(
            src_ref=sbuf.at[step - 1],
            dst_ref=vbuf.at[:, :, own_span, :],
            send_sem=v_send.at[step - 1],
            recv_sem=v_recv.at[step - 1],
            device_id={"ch": ch_peer(step)},
            device_id_type=MESH,
        )
        copy.start()
        v_copies.append(copy)
    p_copies = []
    for step in range(1, bl_count):
        copy = pltpu.make_async_remote_copy(
            src_ref=psend,
            dst_ref=pall.at[bl],
            send_sem=p_send.at[step - 1],
            recv_sem=p_recv.at[step - 1],
            device_id={"bl": lax.rem(bl + step, bl_count)},
            device_id_type=MESH,
        )
        copy.start()
        p_copies.append(copy)
    pall[bl] = psend[...]
    for k in range(2):
        for r in range(2):
            vbuf[k, r, own_span, :] = averaged(own_rows, k, r)

    zero = jnp.zeros((8, LANES), jnp.float32)
    moments = [[zero, zero, zero] for _ in range(2)]
    for first in range(0, half, TILE):
        count = min(TILE, half - first)

        def add_source(row, acc, first=first, count=count):
            span = pl.ds(pl.multiple_of(row * 8, 8), 8)
            fc = [ftab[k, 0, span, :] for k in range(2)]
            fs = [ftab[k, 1, span, :] for k in range(2)]
            out = []
            at = 0
            for d in range(count):
                cd = jnp.broadcast_to(dtab[first + d, 0, pl.ds(row, 1), :], (8, LANES))
                sd = jnp.broadcast_to(dtab[first + d, 1, pl.ds(row, 1), :], (8, LANES))
                for k in range(2):
                    out.append(acc[at] + fc[k] * cd)
                    out.append(acc[at + 1] + fs[k] * sd)
                    out.append(acc[at + 2] + fs[k] * cd)
                    out.append(acc[at + 3] + fc[k] * sd)
                    at += 4
            return tuple(out)

        acc = lax.fori_loop(
            0, slots * sources, add_source, (zero,) * (8 * count), unroll=4
        )
        for d in range(count):
            dist = jnp.float32(first + d + 0.5)
            up = pl.ds(8 * (half + first + d), 8)
            down = pl.ds(8 * (half - 1 - first - d), 8)
            for k in range(2):
                cc, ss, sc, cs = acc[(d * 2 + k) * 4 : (d * 2 + k) * 4 + 4]
                up_r, up_i, dn_r, dn_i = cc - ss, sc + cs, cc + ss, sc - cs
                model[k, 0, up, :] = up_r
                model[k, 1, up, :] = up_i
                model[k, 0, down, :] = dn_r
                model[k, 1, down, :] = dn_i
                up_p = up_r * up_r + up_i * up_i
                dn_p = dn_r * dn_r + dn_i * dn_i
                both = up_p + dn_p
                moments[k][0] = moments[k][0] + both
                moments[k][1] = moments[k][1] + dist * (up_p - dn_p)
                moments[k][2] = moments[k][2] + (dist * dist) * both

    def fold(value):
        return jnp.sum(value, axis=0, keepdims=True)

    for k in range(2):
        a0, a1, a2 = moments[k]
        mall[me, pl.ds(k, 1), :] = fold(a0)
        mall[me, pl.ds(2 + k, 1), :] = fold(omega_c * a0 + omega_step * a1)
        mall[me, pl.ds(4 + k, 1), :] = fold(
            omega_c * omega_c * a0
            + 2.0 * omega_step * omega_c * a1
            + omega_step * omega_step * a2
        )
    mall[me, pl.ds(6, 2), :] = jnp.zeros((2, LANES), jnp.float32)

    def spread(block, send_sem, recv_sem):
        copies = []
        for step in range(1, group):
            copy = pltpu.make_async_remote_copy(
                src_ref=block,
                dst_ref=block,
                send_sem=send_sem.at[step - 1],
                recv_sem=recv_sem.at[step - 1],
                device_id=group_peer(step),
                device_id_type=MESH,
            )
            copy.start()
            copies.append(copy)
        return copies

    m_copies = spread(mall.at[me], m_send, m_recv)

    for copy in p_copies:
        copy.wait()
    station = lax.broadcasted_iota(jnp.int32, (stations, LANES), 0)
    for b in range(bl_count):
        for i in range(2):
            hot = (station == pall[b, pl.ds(i, 1), :]).astype(jnp.float32)
            onehot[:, pl.ds(i * base_all + b * LANES, LANES)] = hot.astype(jnp.bfloat16)

    for copy in v_copies:
        copy.wait()

    stores = [
        pltpu.make_async_copy(vbuf, data_out, out_sem.at[0]),
        pltpu.make_async_copy(model, model_out, out_sem.at[1]),
    ]
    for store in stores:
        store.start()

    for d in range(half):
        up = pl.ds(8 * (half + d), 8)
        down = pl.ds(8 * (half - 1 - d), 8)
        at = pl.ds(8 * d, 8)
        for k in range(2):
            halves = []
            for span in (up, down):
                m_r, m_i = model[k, 0, span, :], model[k, 1, span, :]
                v_r, v_i = vbuf[k, 0, span, :], vbuf[k, 1, span, :]
                halves.append((m_r * v_r + m_i * v_i, m_r * v_i - m_i * v_r))
            (u_r, u_i), (l_r, l_i) = halves
            xtab[k, 0, at, :] = u_r + l_r
            xtab[k, 1, at, :] = u_i + l_i
            xtab[k, 2, at, :] = u_r - l_r
            xtab[k, 3, at, :] = u_i - l_i

    own_first = pl.ds(pl.multiple_of(bl * LANES, LANES), LANES)
    own_second = pl.ds(pl.multiple_of(base_all + bl * LANES, LANES), LANES)
    dist_col = lax.broadcasted_iota(jnp.int32, (half, LANES), 0).astype(jnp.float32) + 0.5

    def own_gain(row):
        return jnp.where(
            pol == 0,
            gathered[pl.ds(row, 1), own_first],
            gathered[pl.ds(row + 1, 1), own_first],
        )

    def delay_tables(k):
        tau = own_gain(4) - gathered[pl.ds(4 + k, 1), own_second]
        sin_d, cos_d = sincos_turns(dist_col * (tau * jnp.float32(8.0 / chans)))
        sin_c, cos_c = sincos_turns(freq_c * tau)
        return sin_d, cos_d, sin_c, cos_c

    gains = (
        jnp.ones((2, stations), jnp.float32),
        jnp.zeros((2, stations), jnp.float32),
        jnp.zeros((2, stations), jnp.float32),
    )
    gathered[pl.ds(0, 2), :] = jnp.ones((2, 2 * base_all), jnp.float32)
    gathered[pl.ds(2, 14), :] = jnp.zeros((14, 2 * base_all), jnp.float32)
    terms[pl.ds(12, 4), :] = jnp.zeros((4, 2 * base_all), jnp.float32)

    for it in range(ITERS):
        for k in range(2):
            if it > 0:
                sin_d, cos_d, sin_c, cos_c = delay_tables(k)
            u_r, u_i, w_r, w_i = zero, zero, zero, zero
            for d in range(half):
                at = pl.ds(8 * d, 8)
                p_r, p_i = xtab[k, 0, at, :], xtab[k, 1, at, :]
                m_r, m_i = xtab[k, 2, at, :], xtab[k, 3, at, :]
                dist = jnp.float32(d + 0.5)
                if it > 0:
                    cd, sd = cos_d[d : d + 1, :], sin_d[d : d + 1, :]
                    u_r = u_r + (cd * p_r + sd * m_i)
                    u_i = u_i + (cd * p_i - sd * m_r)
                    cd, sd = dist * cd, dist * sd
                    w_r = w_r + (cd * m_r + sd * p_i)
                    w_i = w_i + (cd * m_i - sd * p_r)
                else:
                    u_r = u_r + p_r
                    u_i = u_i + p_i
                    w_r = w_r + dist * m_r
                    w_i = w_i + dist * m_i
            w_r = omega_c * u_r + omega_step * w_r
            w_i = omega_c * u_i + omega_step * w_i
            if it > 0:
                u_r, u_i = cos_c * u_r + sin_c * u_i, cos_c * u_i - sin_c * u_r
                w_r, w_i = cos_c * w_r + sin_c * w_i, cos_c * w_i - sin_c * w_r
            for n, value in enumerate((u_r, u_i, w_r, w_i)):
                yall[it, me, pl.ds(2 * n + k, 1), :] = fold(value)
        copies = spread(yall.at[it, me], y_send.at[it], y_recv.at[it])
        if it == 0:
            for copy in m_copies:
                copy.wait()
        for copy in copies:
            copy.wait()

        for b in range(bl_count):
            lane_1 = pl.ds(b * LANES, LANES)
            lane_2 = pl.ds(base_all + b * LANES, LANES)
            uj, wj = gathered[pl.ds(0, 2), lane_2], gathered[pl.ds(2, 2), lane_2]
            nj = uj * uj + wj * wj
            second = [jnp.zeros((2, LANES), jnp.float32)] * 6
            for p in range(pol_count):
                dev = b * pol_count + p
                ui, wi = gathered[pl.ds(p, 1), lane_1], gathered[pl.ds(2 + p, 1), lane_1]
                ni = ui * ui + wi * wi
                y0r, y0i, y1r, y1i = [yall[it, dev, pl.ds(2 * n, 2), :] for n in range(4)]
                p0, p1, p2 = [mall[dev, pl.ds(2 * n, 2), :] for n in range(3)]
                b_r = uj * y1r - wj * y1i
                b_i = uj * y1i + wj * y1r
                cross = ui * b_i - wi * b_r
                s0 = nj * p0
                first = (
                    s0,
                    nj * p1,
                    nj * p2,
                    uj * y0r - wj * y0i - ui * s0,
                    uj * y0i + wj * y0r - wi * s0,
                    cross,
                )
                for x in range(6):
                    terms[pl.ds(2 * x + p, 1), lane_1] = fold(first[x])
                t0 = ni * p0
                more = (
                    t0,
                    ni * p1,
                    ni * p2,
                    ui * y0r + wi * y0i - uj * t0,
                    -(ui * y0i - wi * y0r + wj * t0),
                    -cross,
                )
                second = [a + c for a, c in zip(second, more)]
            for x in range(6):
                terms[pl.ds(2 * x, 2), lane_2] = second[x]

        summed = lax.dot_general(
            split3(terms[...]),
            onehot[...],
            (((1,), (1,)), ((), ())),
            preferred_element_type=jnp.float32,
        )
        summed = summed[0:16] + summed[16:32] + summed[32:48]
        s0, s1, s2, g1, g2, g3 = [summed[2 * x : 2 * x + 2] for x in range(6)]
        u, w, tau = gains
        diagonal = (1.0 + damping) * s0 + 1.0
        cross_r = -w * s1
        cross_i = u * s1
        delay_diag = (1.0 + damping) * (u * u + w * w) * s2 + 1.0
        step_d = (diagonal * g3 - cross_r * g1 - cross_i * g2) / (
            diagonal * delay_diag - cross_r * cross_r - cross_i * cross_i
        )
        step_u = (g1 - cross_r * step_d) / diagonal
        step_w = (g2 - cross_i * step_d) / diagonal
        gains = (u + step_u, w + step_w, tau + step_d)

        rows = jnp.concatenate(
            list(gains) + [jnp.zeros((10, stations), jnp.float32)], axis=0
        )
        got = jnp.dot(split3(rows), onehot[...], preferred_element_type=jnp.float32)
        gathered[...] = got[0:16] + got[16:32] + got[32:48]

    for n in range(3):
        gains_out[n, :, 0, :] = gains[n]

    for k in range(2):
        sin_d, cos_d, sin_c, cos_c = delay_tables(k)
        ui, wi = own_gain(0), own_gain(2)
        uj, wj = gathered[pl.ds(k, 1), own_second], gathered[pl.ds(2 + k, 1), own_second]
        g_r = ui * uj + wi * wj
        g_i = wi * uj - ui * wj
        trig_out[k, 0] = cos_d
        trig_out[k, 1] = sin_d
        turn_out[k, 0] = g_r * cos_c - g_i * sin_c
        turn_out[k, 1] = g_r * sin_c + g_i * cos_c
    for store in stores:
        store.wait()


def residual_kernel(data, model, trig, turn, gains, res_out, gains_out):
    gains_out[...] = gains[...]
    half = trig.shape[2]
    e_r, e_i = turn[0, 0], turn[0, 1]
    for d in range(half):
        cd, sd = trig[0, 0, pl.ds(d, 1), :], trig[0, 1, pl.ds(d, 1), :]
        c_r, c_i, s_r, s_i = e_r * cd, e_i * cd, e_r * sd, e_i * sd
        up = pl.ds(8 * (half + d), 8)
        down = pl.ds(8 * (half - 1 - d), 8)
        for span, f_r, f_i in (
            (up, c_r - s_i, c_i + s_r),
            (down, c_r + s_i, c_i - s_r),
        ):
            m_r, m_i = model[0, 0, span, :], model[0, 1, span, :]
            res_out[0, 0, 0, span, :] = data[0, 0, span, :] - (f_r * m_r - f_i * m_i)
            res_out[0, 1, 0, span, :] = data[0, 1, span, :] - (f_r * m_i + f_i * m_r)


def shards(
    stations, visibility, uv_coords, source_lm, source_flux, avg_factor, station_pairs, slot_owner
):
    ch_count = lax.axis_size("ch")
    bl_count = lax.axis_size("bl")
    pol_count = lax.axis_size("pol")
    slots, chan_local = visibility.shape[2], visibility.shape[3]
    chans = chan_local * ch_count
    sources = source_lm.shape[1]
    half = chans // 16
    group = bl_count * pol_count
    sizes = (ch_count, bl_count, pol_count, slots, chan_local, chans, sources, stations)
    f32 = jnp.float32
    vmem = pl.BlockSpec(memory_space=pltpu.VMEM)
    smem = pl.BlockSpec(memory_space=pltpu.SMEM)
    dma = pltpu.SemaphoreType.DMA
    anywhere = pl.BlockSpec(memory_space=pl.ANY)
    solved = pl.pallas_call(
        functools.partial(kernel, sizes),
        out_shape=(
            jax.ShapeDtypeStruct((2, 2, chans, LANES), f32),
            jax.ShapeDtypeStruct((2, 2, chans, LANES), f32),
            jax.ShapeDtypeStruct((2, 2, half, LANES), f32),
            jax.ShapeDtypeStruct((2, 2, 8, LANES), f32),
            jax.ShapeDtypeStruct((3, 2, 1, stations), f32),
        ),
        in_specs=[pl.BlockSpec(memory_space=pl.ANY), vmem, smem, smem, vmem, vmem, smem],
        out_specs=(anywhere, anywhere, vmem, vmem, vmem),
        scratch_shapes=[
            pltpu.VMEM((2, 2, chans, LANES), f32),
            pltpu.VMEM((ch_count - 1, 2, 2, chan_local, LANES), f32),
            pltpu.VMEM((2, 2, chans, LANES), f32),
            pltpu.VMEM((slots * sources, LANES), f32),
            pltpu.VMEM((2, 2, slots * sources * 8, LANES), f32),
            pltpu.VMEM((half, 2, slots * sources, LANES), f32),
            pltpu.VMEM((2, 4, half * 8, LANES), f32),
            pltpu.VMEM((8, LANES), jnp.int32),
            pltpu.VMEM((bl_count, 8, LANES), jnp.int32),
            pltpu.VMEM((group, 8, LANES), f32),
            pltpu.VMEM((ITERS, group, 8, LANES), f32),
            pltpu.VMEM((stations, 2 * bl_count * LANES), jnp.bfloat16),
            pltpu.VMEM((16, 2 * bl_count * LANES), f32),
            pltpu.VMEM((16, 2 * bl_count * LANES), f32),
            dma((ch_count - 1,)),
            dma((ch_count - 1,)),
            dma((bl_count - 1,)),
            dma((bl_count - 1,)),
            dma((group - 1,)),
            dma((group - 1,)),
            dma((ITERS, group - 1)),
            dma((ITERS, group - 1)),
            pltpu.VMEM(visibility.shape, f32),
            dma,
            dma((2,)),
        ],
        compiler_params=pltpu.CompilerParams(
            collective_id=0, has_side_effects=True, vmem_limit_bytes=56 * 1024 * 1024
        ),
    )(
        visibility,
        uv_coords,
        source_lm,
        source_flux,
        avg_factor.reshape(1, -1),
        station_pairs,
        slot_owner,
    )
    rows = pl.BlockSpec((1, 2, chans, LANES), lambda k: (k, 0, 0, 0))
    gain_spec = pl.BlockSpec((3, 2, 1, stations), lambda k: (0, 0, 0, 0))
    return pl.pallas_call(
        residual_kernel,
        grid=(2,),
        out_shape=(
            jax.ShapeDtypeStruct((2, 2, 1, chans, LANES), f32),
            jax.ShapeDtypeStruct((3, 2, 1, stations), f32),
        ),
        in_specs=[
            rows,
            rows,
            pl.BlockSpec((1, 2, half, LANES), lambda k: (k, 0, 0, 0)),
            pl.BlockSpec((1, 2, 8, LANES), lambda k: (k, 0, 0, 0)),
            gain_spec,
        ],
        out_specs=(
            pl.BlockSpec((1, 2, 1, chans, LANES), lambda k: (k, 0, 0, 0, 0)),
            gain_spec,
        ),
        compiler_params=pltpu.CompilerParams(vmem_limit_bytes=60 * 1024 * 1024),
    )(*solved)


def solution(mesh):
    placed = (
        P("pol", None, None, "ch", ("grp", "bl")),
        P(None, None, ("grp", "bl")),
        P(),
        P("pol", None),
        P(("grp", "bl")),
        P(None, ("grp", "bl")),
        P(),
    )
    return jax.shard_map(
        functools.partial(shards, 512),
        mesh=mesh,
        in_specs=placed,
        out_specs=(P("pol", None, "ch", None, ("grp", "bl")), P(None, None, "ch", "grp")),
        check_vma=False,
    )
```
